256 devices in a mesh: seq: 32 (over z, y), vocab: 8 (over x, core).
Axes of the slice: x: 4, y: 4, z: 8, core: 2. Of those that a mesh axis runs over, the one named last changes fastest.
Arguments:
- queries: bfloat16 [512, 8192], P('seq'), may hold values from -200 to 200
- span_keys: bfloat16 [512, 1024], P('seq'), may hold values from -3 to 3
- span_head_values: bfloat16 [512, 1024], P('seq'), may hold values from -24 to 24
- prefix_cached_keys: bfloat16 [65536, 1024], P(('seq', 'vocab')), may hold values from -6 to 6
- prefix_cached_values: bfloat16 [65536, 1024], P(('seq', 'vocab')), may hold values from -24 to 24
- start: int32 [1], replicated, may hold values from 32768 to 65536
- out_weight: bfloat16 [8192, 8192], P('seq', 'vocab'), may hold values from -0.25 to 0.25
- residual: bfloat16 [512, 8192], P('seq', 'vocab')
- norm_gain: float32 [8192], P('vocab'), may hold values from 0.5 to 1.5
- head_weight: bfloat16 [8192, 65536], P('vocab', 'seq')
- targets: int32 [512], P('vocab'), may hold values from 0 to 65535
Outputs:
- hidden: bfloat16 [512, 8192], P('seq', 'vocab')
- logprobs: float32 [512], P('vocab')
The draws below stay inside these ranges and needn't reach their ends.
Inputs may be any that keep to these rules, and one draw needn't show every extreme that they name: The span's tokens follow the first start cache positions of this sequence.
All inputs are finite; a program needn't handle non-finite values.
Results may differ from the reference program's by a relative error of at most 0.023.
Values may be sent and summed in bfloat16 or wider, within the bound.
A program may use at most 64 MiB of HBM per device.

```python
import math
import jax
import jax.numpy as jnp
import numpy as np
from jax import lax

D = 8192
QUERY_HEADS = 64
KEY_VALUE_HEADS = 8
HEAD_SIZE = 128
VOCAB = 65536
SPAN_TOKENS = 512
CACHE_POSITIONS = 65536


def shared_keys(key):
    return jnp.clip(jax.random.normal(key, (SPAN_TOKENS, KEY_VALUE_HEADS * HEAD_SIZE), jnp.float32), -3.0, 3.0)


def paired_rows(sampled_keys, factor):
    row_total = sampled_keys.shape[0]
    positions = jnp.arange(row_total)
    chosen = positions % 11 == 7
    before = jnp.roll(chosen, -1)
    following = jnp.roll(sampled_keys, -1, axis=0)
    return (jnp.where(before[:, None], factor * following, sampled_keys), chosen)


def drawn_directions(key):
    return jnp.clip(jax.random.normal(key, (8, D), jnp.float32), -3.0, 3.0)


def feature_ramp():
    return jnp.exp(math.log(10.0) * (jnp.arange(D, dtype=jnp.float32) / D - 0.5))


def draw_span_keys(key, part):
    sampled_keys = shared_keys(key)
    sampled_keys, chosen = paired_rows(sampled_keys, 0.99)
    return sampled_keys.astype(jnp.bfloat16)


def draw_queries(key, part):
    sampled_keys = shared_keys(key)
    key = jax.random.fold_in(key, 5)
    values = 2.0 * jnp.clip(jax.random.normal(key, (SPAN_TOKENS, QUERY_HEADS * HEAD_SIZE), jnp.float32), -3.0, 3.0)
    sampled_keys, chosen = paired_rows(sampled_keys, 0.99)
    positions = jnp.arange(SPAN_TOKENS)
    strength = jnp.array([9.0, 14.0, 20.0], jnp.float32)[positions // 11 % 3]
    head_replicas = jnp.broadcast_to(sampled_keys.reshape(SPAN_TOKENS, KEY_VALUE_HEADS, 1, HEAD_SIZE), (SPAN_TOKENS, KEY_VALUE_HEADS, QUERY_HEADS // KEY_VALUE_HEADS, HEAD_SIZE)).reshape(SPAN_TOKENS, QUERY_HEADS * HEAD_SIZE)
    values = jnp.where(chosen[:, None], strength[:, None] * head_replicas, values)
    return values.astype(jnp.bfloat16)


def draw_head_weight(key, part):
    directions = drawn_directions(key)
    key = jax.random.fold_in(key, 17)
    weights = 3.0 / math.sqrt(D) * jnp.clip(jax.random.normal(key, (D, VOCAB), jnp.float32), -4.0, 4.0)
    boost = 3.0 / math.sqrt(D)
    moved = jnp.roll(directions, 4, axis=0)
    columns = np.arange(8) * (VOCAB // 8) + 7
    weights = weights.at[:, columns].set(boost * moved.T)
    weights = weights.at[:, columns + 1].set(0.99 * boost * moved.T)
    return weights.astype(jnp.bfloat16)


def draw_residual(key, part):
    directions = drawn_directions(key)
    key = jax.random.fold_in(key, 23)
    part_a, part_b, part_c = jax.random.split(key, 3)
    standard = jnp.clip(jax.random.normal(part_a, (SPAN_TOKENS, D), jnp.float32), -3.0, 3.0)
    row_scale = jnp.exp(jax.random.uniform(part_b, (SPAN_TOKENS, 1), jnp.float32, -1.15, 1.15))
    column_ramp = feature_ramp()
    col_scale = jnp.exp(jax.random.uniform(part_c, (1, D), jnp.float32, -0.7, 0.7)) * column_ramp[None, :]
    values = 0.8 * standard * row_scale * col_scale
    row_ids = (np.arange(8) * (SPAN_TOKENS // 8) + 1) % SPAN_TOKENS
    strengths = jnp.array([0.6, 1.0, 4.0, 0.6, 1.0, 4.0, 0.6, 1.0], jnp.float32)[:, None]
    values = values.at[row_ids].set((strengths * directions + standard[row_ids]) * column_ramp[None, :])
    return values.astype(jnp.bfloat16)


def with_ends(entries, key, low, top_value):
    extent = entries.shape
    index_at = [jax.random.randint(jax.random.fold_in(key, axis), (), 0, extent[axis]) for axis in range(len(extent))]
    entries = entries.at[tuple(index_at)].set(low)
    longest = extent.index(max(extent))
    index_at[longest] = (index_at[longest] + 1) % extent[longest]
    return entries.at[tuple(index_at)].set(top_value)


def levels(key, extent, cuts, least, top_value):
    gain, own = 1.0, jax.random.fold_in(key, 6)
    for position, blocks in cuts:
        draws = jnp.exp(jax.random.uniform(jax.random.fold_in(own, position), (blocks,), jnp.float32, least / len(cuts), top_value / len(cuts)))
        gain = gain * jnp.repeat(draws, extent[position] // blocks).reshape([-1 if axis == position else 1 for axis in range(len(extent))])
    return gain


def scatter_about(own_key, dims, scale, reach, pieces=(), held_as=jnp.bfloat16):
    values = scale * jax.random.normal(own_key, dims, jnp.float32)
    if pieces:
        values = values * levels(own_key, dims, pieces, -0.22, 0.18)
    return jnp.clip(values, -reach, reach).astype(held_as)


def setup_inputs(seed: int = 0) -> dict:
    streams_of = jax.random.split(jax.random.key(seed), 12)
    return {
        "queries": draw_queries(jax.random.fold_in(streams_of[11], 71), 0),
        "span_keys": draw_span_keys(jax.random.fold_in(streams_of[11], 71), 0),
        "span_head_values": scatter_about(streams_of[2], (SPAN_TOKENS, KEY_VALUE_HEADS * HEAD_SIZE), 4.0, 24.0, ((0, 32),)),
        "prefix_cached_keys": scatter_about(streams_of[3], (CACHE_POSITIONS, KEY_VALUE_HEADS * HEAD_SIZE), 1.0, 6.0, ((0, 256),)),
        "prefix_cached_values": scatter_about(streams_of[4], (CACHE_POSITIONS, KEY_VALUE_HEADS * HEAD_SIZE), 4.0, 24.0, ((0, 256),)),
        "start": jax.random.randint(streams_of[5], (1,), CACHE_POSITIONS // 2, CACHE_POSITIONS + 1).astype(jnp.int32),
        "out_weight": scatter_about(streams_of[6], (QUERY_HEADS * HEAD_SIZE, D), (4 * HEAD_SIZE) ** -0.5, 0.25, ((0, 32), (1, 8))),
        "residual": draw_residual(jax.random.fold_in(streams_of[11], 71), 0),
        "norm_gain": jnp.clip(1.0 + 0.1 * jax.random.normal(streams_of[8], (D,), jnp.float32), 0.5, 1.5),
        "head_weight": draw_head_weight(jax.random.fold_in(streams_of[11], 71), 0),
        "targets": with_ends(jax.random.randint(streams_of[10], (SPAN_TOKENS,), 0, VOCAB), jax.random.fold_in(streams_of[10], 1), 0, VOCAB - 1).astype(jnp.int32),
    }


NEG_FILL = -1e+30
EPSILON = 1e-05

def reference(queries, span_keys, span_head_values, prefix_cached_keys, prefix_cached_values, start, out_weight, residual, norm_gain, head_weight, targets):
    query_group_size = QUERY_HEADS // KEY_VALUE_HEADS
    score_scale = 1.0 / math.sqrt(HEAD_SIZE)
    live_count = start[0]
    cache_ok = jnp.arange(CACHE_POSITIONS, dtype=jnp.int32) < live_count
    token_ids = jnp.arange(SPAN_TOKENS, dtype=jnp.int32)
    causal = token_ids[None, :] <= token_ids[:, None]

    def one_head(head_id):
        kv_id = head_id // query_group_size
        query_rows = lax.dynamic_slice_in_dim(queries, (head_id * HEAD_SIZE).astype(jnp.int32), HEAD_SIZE, 1)
        cache_k = lax.dynamic_slice_in_dim(prefix_cached_keys, (kv_id * HEAD_SIZE).astype(jnp.int32), HEAD_SIZE, 1)
        cache_v = lax.dynamic_slice_in_dim(prefix_cached_values, (kv_id * HEAD_SIZE).astype(jnp.int32), HEAD_SIZE, 1)
        span_k = lax.dynamic_slice_in_dim(span_keys, (kv_id * HEAD_SIZE).astype(jnp.int32), HEAD_SIZE, 1)
        span_v = lax.dynamic_slice_in_dim(span_head_values, (kv_id * HEAD_SIZE).astype(jnp.int32), HEAD_SIZE, 1)
        cache_scores = jnp.dot(query_rows, cache_k.T, preferred_element_type=jnp.float32) * score_scale
        span_scores = jnp.dot(query_rows, span_k.T, preferred_element_type=jnp.float32) * score_scale
        cache_scores = jnp.where(cache_ok[None, :], cache_scores, NEG_FILL)
        span_scores = jnp.where(causal, span_scores, NEG_FILL)
        row_peak = jnp.maximum(lax.optimization_barrier(jnp.max(cache_scores, axis=1)), lax.optimization_barrier(jnp.max(span_scores, axis=1)))
        cache_probs = jnp.where(cache_ok[None, :], jnp.exp(cache_scores - row_peak[:, None]), 0.0)
        span_probs = jnp.where(causal, jnp.exp(span_scores - row_peak[:, None]), 0.0)
        row_total = lax.optimization_barrier(jnp.sum(cache_probs, axis=1)) + lax.optimization_barrier(jnp.sum(span_probs, axis=1))
        weighted = jnp.dot(cache_probs.astype(jnp.bfloat16), cache_v, preferred_element_type=jnp.float32)
        weighted = weighted + jnp.dot(span_probs.astype(jnp.bfloat16), span_v, preferred_element_type=jnp.float32)
        return (weighted / row_total[:, None]).astype(jnp.bfloat16)
    per_head = lax.map(one_head, jnp.arange(QUERY_HEADS, dtype=jnp.int32))
    attended = jnp.transpose(per_head, (1, 0, 2)).reshape(SPAN_TOKENS, QUERY_HEADS * HEAD_SIZE)
    projected = jnp.dot(attended, out_weight, preferred_element_type=jnp.float32)
    hidden = (residual.astype(jnp.float32) + projected).astype(jnp.bfloat16)
    widened = hidden.astype(jnp.float32)
    mean_square = lax.optimization_barrier(jnp.mean(widened * widened, axis=1))
    normed = (widened * lax.rsqrt(mean_square + EPSILON)[:, None] * norm_gain[None, :]).astype(jnp.bfloat16)
    logits = jnp.dot(normed, head_weight, preferred_element_type=jnp.float32)
    row_peak = lax.optimization_barrier(jnp.max(logits, axis=1))
    log_total = row_peak + jnp.log(lax.optimization_barrier(jnp.sum(jnp.exp(logits - row_peak[:, None]), axis=1)))
    picked = jnp.take_along_axis(logits, targets[:, None].astype(jnp.int32), axis=1)[:, 0]
    return (hidden, picked - log_total)
```

```python
import functools
import math

import jax
import jax.numpy as jnp
from jax import lax
from jax.experimental import pallas as pl
from jax.experimental.pallas import tpu as pltpu
from jax.sharding import PartitionSpec as P

D = 8192
HEADS = 8
HS = 128
NY, NZ, NX = 4, 8, 4
NV = 2 * NX
ROWS = 16
CACHE = 256
KEYS = NV * CACHE
KEYS_PAD = KEYS + 128
GW = HEADS * HS
PW = GW + 128
VOC = 2048
TILE = 512
NT = VOC // TILE
FEAT = 256
BIG_NEG = -1e30
EPSILON = 1e-05
MESH = pl.DeviceIdType.MESH
BF = jnp.bfloat16
F32 = jnp.float32


class Place:
    def __init__(self):
        s, v = lax.axis_index("seq"), lax.axis_index("vocab")
        self.s, self.v = s, v
        self.z, self.y = lax.div(s, NY), lax.rem(s, NY)
        self.x, self.c = lax.div(v, 2), lax.rem(v, 2)

    def yy(self, d):
        return lax.rem(self.y + d + NY, NY)

    def zz(self, d):
        return lax.rem(self.z + d + NZ, NZ)

    def xx(self, d):
        return lax.rem(self.x + d + NX, NX)

    def at_z(self, d):
        return (self.zz(d) * NY + self.y, self.v)

    def at_y(self, d):
        return (self.z * NY + self.yy(d), self.v)

    def at_x(self, d, core):
        return (self.s, self.xx(d) * 2 + core)

    def at_v(self, d):
        return (self.s, lax.rem(self.v + d, NV))


def rdma(src, dst, send, recv, dev):
    return pltpu.make_async_remote_copy(
        src_ref=src, dst_ref=dst, send_sem=send, recv_sem=recv, device_id=dev, device_id_type=MESH
    )


def greet(partners, extra=()):
    bar = pltpu.get_barrier_semaphore()
    for dev in partners:
        pl.semaphore_signal(bar, inc=1, device_id=dev, device_id_type=MESH)
    count = len(partners)
    for use, dev in extra:

        @pl.when(use)
        def _():
            pl.semaphore_signal(bar, inc=1, device_id=dev, device_id_type=MESH)

        count = count + use.astype(jnp.int32)
    pl.semaphore_wait(bar, count)


def seq_partners(me):
    return [me.at_z(d) for d in range(1, NZ)] + [me.at_y(1), me.at_y(-1)]


def gather_seq(me, buf, zs, zr, ys, yr, fs, fr):
    half = buf.shape[3] // 2
    sends = []

    def go(cp):
        cp.start()
        sends.append(cp)

    own = buf.at[me.y, me.z]
    for d in range(1, NZ):
        go(rdma(own, own, zs.at[d - 1], zr.at[d - 1], me.at_z(d)))
    for step in range(NZ + 1):
        if step < NZ:
            zz = me.zz(-step)
            blk = buf.at[me.y, zz]
            if step:
                rdma(blk, blk, zs.at[step - 1], zr.at[step - 1], me.at_z(1)).wait_recv()
            go(rdma(blk, blk, ys.at[0, step], yr.at[0, step], me.at_y(1)))
            go(rdma(blk, blk, ys.at[1, step], yr.at[1, step], me.at_y(-1)))
        if step:
            d = step - 1
            zz = me.zz(-d)
            for k, way in ((0, 1), (1, -1)):
                blk = buf.at[me.yy(-way), zz]
                rdma(blk, blk, ys.at[k, d], yr.at[k, d], me.at_y(way)).wait_recv()
                part = buf.at[me.yy(-way), zz, :, pl.ds(k * half, half)]
                go(rdma(part, part, fs.at[k, d], fr.at[k, d], me.at_y(way)))
    for d in range(NZ):
        zz = me.zz(-d)
        for k in range(2):
            part = buf.at[me.yy(2), zz, :, pl.ds(k * half, half)]
            rdma(part, part, fs.at[k, d], fr.at[k, d], me.at_y(1)).wait_recv()
    return sends


GATHER_SEMS = [
    pltpu.SemaphoreType.DMA((NZ - 1,)),
    pltpu.SemaphoreType.DMA((NZ - 1,)),
    pltpu.SemaphoreType.DMA((2, NZ)),
    pltpu.SemaphoreType.DMA((2, NZ)),
    pltpu.SemaphoreType.DMA((2, NZ)),
    pltpu.SemaphoreType.DMA((2, NZ)),
]


def reduce_seq(me, part, r1, r2, mg, rz, ss, rs, zs, zr, join, last):
    width = part.shape[3]
    hz = NZ // 2
    sends = []

    def go(cp):
        cp.start()
        sends.append(cp)

    far = me.yy(2)
    for k, way in ((0, 1), (1, -1)):
        half = pl.ds(k * hz, hz)
        go(rdma(part.at[far, half], r1.at[k], ss.at[k, 0], rs.at[k, 0], me.at_y(way)))
    for k, way in ((0, 1), (1, -1)):
        other = pl.ds((1 - k) * hz, hz)
        go(rdma(part.at[me.yy(way), other], r2.at[k, other], ss.at[k, 1], rs.at[k, 1], me.at_y(way)))
    for k, way in ((0, 1), (1, -1)):
        rdma(r1.at[k], r1.at[k], ss.at[k, 0], rs.at[k, 0], me.at_y(way)).wait_recv()
        half = pl.ds(k * hz, hz)
        mine = part[me.yy(way), half].reshape(hz * ROWS, width)
        got = r1[k].reshape(hz * ROWS, width)
        part[me.yy(way), half] = join([mine, got]).reshape(hz, ROWS, width)
        go(rdma(part.at[me.yy(way), half], r2.at[k, half], ss.at[k, 2], rs.at[k, 2], me.at_y(way)))
    for k, way in ((0, 1), (1, -1)):
        for i in range(2):
            half = pl.ds((k if i else 1 - k) * hz, hz)
            blk = r2.at[k, half]
            rdma(blk, blk, ss.at[k, 1 + i], rs.at[k, 1 + i], me.at_y(way)).wait_recv()
    items = [part[me.y].reshape(NZ * ROWS, width)]
    items += [r2[k].reshape(NZ * ROWS, width) for k in range(2)]
    mg[...] = join(items).reshape(NZ, ROWS, width)
    for d in range(1, NZ):
        go(rdma(mg.at[me.zz(d)], rz.at[d - 1], zs.at[d - 1], zr.at[d - 1], me.at_z(d)))
    items = [mg[me.z]]
    for d in range(1, NZ):
        blk = rz.at[d - 1]
        rdma(blk, blk, zs.at[d - 1], zr.at[d - 1], me.at_z(d)).wait_recv()
        items.append(rz[d - 1])
    return last(items), sends


def reduce_scratch(width):
    return [
        pltpu.VMEM((2, NZ // 2, ROWS, width), BF),
        pltpu.VMEM((2, NZ, ROWS, width), BF),
        pltpu.VMEM((NZ, ROWS, width), BF),
        pltpu.VMEM((NZ - 1, ROWS, width), BF),
        pltpu.SemaphoreType.DMA((2, 3)),
        pltpu.SemaphoreType.DMA((2, 3)),
        pltpu.SemaphoreType.DMA((NZ - 1,)),
        pltpu.SemaphoreType.DMA((NZ - 1,)),
    ]


def lanes(shape):
    return lax.broadcasted_iota(jnp.int32, shape, len(shape) - 1)


def pack_lse(lse, low8):
    second = pltpu.roll(lse, 8, 1) if low8 else lse
    third = pltpu.roll(lse, 16, 1) if low8 else lse

    def split(a):
        hi = a.astype(BF).astype(F32)
        mid = (a - hi).astype(BF).astype(F32)
        return hi, mid, a - hi - mid

    lane = lanes(lse.shape)
    out = jnp.where(lane < 8, split(lse)[0], jnp.where(lane < 16, split(second)[1], split(third)[2]))
    return jnp.where(lane < 24, out, 0.0).astype(BF)


def unpack_lse(packed):
    a = packed.astype(F32)
    return a + (pltpu.roll(a, 120, 1) + pltpu.roll(a, 112, 1))


def join_partials(items, final=False):
    lses = [unpack_lse(it[:, GW:]) for it in items]
    peak = functools.reduce(jnp.maximum, lses)
    weights = [jnp.exp2(l - peak) for l in lses]
    total = functools.reduce(jnp.add, weights)
    weights = [w / total for w in weights]
    cols = []
    for h in range(HEADS):
        acc = None
        for w, it in zip(weights, items):
            term = w[:, h : h + 1] * it[:, h * HS : (h + 1) * HS].astype(F32)
            acc = term if acc is None else acc + term
        cols.append(acc.astype(BF))
    if not final:
        cols.append(pack_lse(peak + jnp.log2(total), True))
    return jnp.concatenate(cols, axis=1)


def attention_kernel(
    q_ref, sk_ref, sv_ref, ck_ref, cv_ref, start_ref, out_ref,
    qall, kbuf, vbuf, vext, krel, vrel, bias, lse_buf, opart,
    gz, gzr, gy, gyr, gf, gfr, loc, kvs, kr, vr, rels, relr, fws,
    r1, r2, mg, rz, rss, rsr, rzs, rzr,
):
    me = Place()
    sends = []

    def go(cp):
        cp.start()
        sends.append(cp)

    head_cols = pl.ds(pl.multiple_of(me.v * GW, GW), GW)
    own_q = pltpu.make_async_copy(q_ref.at[:, head_cols], qall.at[me.y, me.z], loc.at[0])
    own_q.start()

    def cols(vv):
        return pl.ds(pl.multiple_of(vv * HS, HS), HS)

    def rows(vv):
        return pl.ds(pl.multiple_of(vv * CACHE, CACHE), CACHE)

    own_k = pltpu.make_async_copy(ck_ref.at[:, cols(me.v)], kbuf.at[rows(me.v)], kr.at[me.v])
    own_v = pltpu.make_async_copy(cv_ref.at[:, cols(me.v)], vbuf.at[rows(me.v)], vr.at[me.v])
    own_k.start()
    own_v.start()
    kbuf[KEYS:, :] = jnp.zeros((128, HS), BF)
    vbuf[KEYS:, :] = jnp.zeros((128, HS), BF)
    kbuf[KEYS : KEYS + ROWS, :] = sk_ref[:, cols(me.v)]
    vbuf[KEYS : KEYS + ROWS, :] = sv_ref[:, cols(me.v)]
    own_q.wait()
    near = [(0, 1 - me.c), (1, 0), (1, 1), (-1, 0), (-1, 1)]
    greet(seq_partners(me) + [me.at_x(d, c) for d, c in near])

    farx = me.xx(2)
    far_cols = pl.ds(pl.multiple_of(farx * 2 * HS, 2 * HS), 2 * HS)
    go(rdma(ck_ref.at[:, far_cols], krel, rels.at[0], relr.at[0], me.at_x(1, me.c)))
    go(rdma(cv_ref.at[:, far_cols], vrel, rels.at[1], relr.at[1], me.at_x(-1, me.c)))
    for i, (d, c) in enumerate(near):
        vv = me.xx(d) * 2 + c
        go(rdma(ck_ref.at[:, cols(vv)], kbuf.at[rows(me.v)], kvs.at[0, i], kr.at[me.v], me.at_x(d, c)))
        go(rdma(cv_ref.at[:, cols(vv)], vbuf.at[rows(me.v)], kvs.at[1, i], vr.at[me.v], me.at_x(d, c)))

    sends += gather_seq(me, qall, gz, gzr, gy, gyr, gf, gfr)

    rdma(krel, krel, rels.at[0], relr.at[0], me.at_x(1, me.c)).wait_recv()
    src = me.xx(-1) * 2 + me.c
    for c in range(2):
        go(rdma(krel.at[:, pl.ds(c * HS, HS)], kbuf.at[rows(src)], fws.at[0, c], kr.at[src], me.at_x(1, c)))
    rdma(vrel, vrel, rels.at[1], relr.at[1], me.at_x(-1, me.c)).wait_recv()
    src = me.xx(1) * 2 + me.c
    for c in range(2):
        go(rdma(vrel.at[:, pl.ds(c * HS, HS)], vbuf.at[rows(src)], fws.at[1, c], vr.at[src], me.at_x(-1, c)))

    flat = lanes((1, KEYS_PAD))
    bias[...] = jnp.where(flat < start_ref[0] - me.s * KEYS, 0.0, BIG_NEG)
    own_k.wait()
    own_v.wait()
    for d in range(1, NV):
        src = lax.rem(me.v + d, NV)
        blk = kbuf.at[rows(src)]
        rdma(blk, blk, kvs.at[0, 0], kr.at[src], me.at_v(1)).wait_recv()
        blk = vbuf.at[rows(src)]
        rdma(blk, blk, kvs.at[1, 0], vr.at[src], me.at_v(1)).wait_recv()
    vext[:, :HS] = vbuf[...]
    vext[:, HS:] = jnp.ones((KEYS_PAD, HS), BF)

    scale = math.log2(math.e) / math.sqrt(HS)
    nrow = NZ * ROWS
    for order in (2, 1, 3, 0):
        yy = me.yy(order)

        def pair(hp, carry):
            both = []
            for i in range(2):
                at = pl.ds(pl.multiple_of((hp * 2 + i) * HS, HS), HS)
                both.append(qall[yy, :, :, at].reshape(nrow, HS))
            q2 = jnp.concatenate(both, axis=0)
            sc = lax.dot_general(q2, kbuf[...], (((1,), (1,)), ((), ())), preferred_element_type=F32)
            main = sc[:, :KEYS] * scale + bias[:, :KEYS]
            row = lax.broadcasted_iota(jnp.int32, (2 * nrow, 128), 0)
            row = lax.rem(row, nrow)
            token = lax.div(row, ROWS) * (NY * ROWS) + yy * ROWS + lax.rem(row, ROWS)
            key = lanes((2 * nrow, 128))
            ok = (key < ROWS) & (key + me.s * ROWS <= token)
            span = jnp.where(ok, sc[:, KEYS:] * scale, BIG_NEG)
            peak = jnp.maximum(
                jnp.max(main, axis=1, keepdims=True), jnp.max(span, axis=1, keepdims=True)
            )
            pm = jnp.exp2(main - peak).astype(BF)
            ps = jnp.exp2(span - peak).astype(BF)
            ps = jnp.where(ok, ps, jnp.zeros_like(ps))
            o = jnp.dot(pm, vext[:KEYS, :], preferred_element_type=F32)
            o = o + jnp.dot(ps, vext[KEYS:, :], preferred_element_type=F32)
            total = o[:, HS:]
            total = jnp.where(total > 0.0, total, 1.0)
            on = (o[:, :HS] / total).astype(BF)
            lse = peak + jnp.log2(total)
            lane = lanes((nrow, 128))
            for i in range(2):
                h = hp * 2 + i
                at = pl.ds(pl.multiple_of(h * HS, HS), HS)
                opart[yy, :, :, at] = on[i * nrow : (i + 1) * nrow].reshape(NZ, ROWS, HS)
                mine = lse[i * nrow : (i + 1) * nrow]
                lse_buf[...] = jnp.where(lax.rem(lane, 8) == h, mine, lse_buf[...])
            return carry

        lax.fori_loop(0, HEADS // 2, pair, 0)
        opart[yy, :, :, GW:] = pack_lse(lse_buf[...], False).reshape(NZ, ROWS, 128)

    joined, more = reduce_seq(
        me, opart, r1, r2, mg, rz, rss, rsr, rzs, rzr,
        join_partials, functools.partial(join_partials, final=True),
    )
    out_ref[...] = joined
    for cp in sends + more:
        cp.wait_send()


def add_partials(items):
    return functools.reduce(jnp.add, [it.astype(F32) for it in items]).astype(BF)


def add_last(items):
    return functools.reduce(jnp.add, [it.astype(F32) for it in items])


def project_kernel(
    att_ref, w_ref, res_ref, gain_ref, hid_ref, nall_ref,
    tin, aall, opart, sq, nall, tss, trs, avs, avr, sqs, sqr,
    gz, gzr, gy, gyr, gf, gfr,
    r1, r2, mg, rz, rss, rsr, rzs, rzr,
):
    me = Place()
    sends = []

    def go(cp):
        cp.start()
        sends.append(cp)

    same = [(me.z == me.v) & (me.y == j) for j in range(NY)]
    across = [(me.v * NY + j, me.z) for j in range(NY)]
    greet(
        seq_partners(me) + [me.at_v(d) for d in range(1, NV)],
        [(jnp.logical_not(same[j]), across[j]) for j in range(NY)],
    )

    turns = []
    for j in range(NY):
        src = att_ref.at[:, pl.ds(j * FEAT, FEAT)]
        cp = rdma(src, tin.at[me.y], tss.at[j], trs.at[me.y], across[j])
        loc = pltpu.make_async_copy(src, tin.at[me.y], trs.at[me.y])

        @pl.when(jnp.logical_not(same[j]))
        def _():
            cp.start()

        @pl.when(same[j])
        def _():
            loc.start()

        turns.append((jnp.logical_not(same[j]), cp))
    for j in range(NY):
        blk = tin.at[j]
        rdma(blk, blk, tss.at[j], trs.at[j], across[0]).wait_recv()
    aall[me.v] = tin[...]
    for d in range(1, NV):
        go(rdma(tin, aall.at[me.v], avs.at[d - 1], avr.at[d - 1], me.at_v(d)))
    for d in range(1, NV):
        blk = aall.at[lax.rem(me.v - d + NV, NV)]
        rdma(blk, blk, avs.at[d - 1], avr.at[d - 1], me.at_v(1)).wait_recv()

    nrow = NZ * ROWS
    for order in (2, 1, 3, 0):
        yy = me.yy(order)
        a = aall[:, yy].reshape(nrow, FEAT)
        opart[yy] = jnp.dot(a, w_ref[...], preferred_element_type=F32).astype(BF).reshape(NZ, ROWS, GW)
    projected, more = reduce_seq(
        me, opart, r1, r2, mg, rz, rss, rsr, rzs, rzr, add_partials, add_last
    )
    sends += more
    hidden = (res_ref[...].astype(F32) + projected).astype(BF)
    hid_ref[...] = hidden
    wide = hidden.astype(F32)
    sq[me.v] = jnp.broadcast_to(jnp.sum(wide * wide, axis=1, keepdims=True), (ROWS, 128))
    for d in range(1, NV):
        go(rdma(sq.at[me.v], sq.at[me.v], sqs.at[d - 1], sqr.at[d - 1], me.at_v(d)))
    for d in range(1, NV):
        blk = sq.at[lax.rem(me.v - d + NV, NV)]
        rdma(blk, blk, sqs.at[d - 1], sqr.at[d - 1], me.at_v(1)).wait_recv()
    mean = jnp.sum(sq[...], axis=0)[:, :1] * (1.0 / D)
    nall[me.y, me.z] = (wide * lax.rsqrt(mean + EPSILON) * gain_ref[...]).astype(BF)
    sends += gather_seq(me, nall, gz, gzr, gy, gyr, gf, gfr)
    nall_ref[...] = nall[...]
    for use, cp in turns:

        @pl.when(use)
        def _():
            cp.wait_send()

    for cp in sends:
        cp.wait_send()


def logits_kernel(
    n_ref, hw_ref, tgt_ref, out_ref,
    osend, orecv, own, sx, x1, x2, sty, stz, cs, cr, xs, xr, yss, yrs, zss, zrs,
):
    me = Place()
    sends = []

    def go(cp):
        cp.start()
        sends.append(cp)

    greet(
        [me.at_z(d) for d in range(1, NZ)]
        + [me.at_y(d) for d in range(1, NY)]
        + [me.at_x(0, 1 - me.c), me.at_x(1, me.c), me.at_x(-1, me.c)]
    )
    tok = NY * ROWS
    shift = (2, 1, 3, 0)

    def rows_of(core):
        blocks = []
        for d in shift:
            for y in range(NY):
                blocks.append(n_ref[y, me.xx(d) * 2 + core])
        return jnp.concatenate(blocks, axis=0)

    sib = me.at_x(0, 1 - me.c)
    lhs = rows_of(1 - me.c)
    for n in range(NT):
        at = pl.ds(n * TILE, TILE)
        osend[n] = (
            jnp.dot(lhs, hw_ref[:, at], preferred_element_type=F32).astype(BF).reshape(NX, tok, TILE)
        )
        go(rdma(osend.at[n], orecv.at[n], cs.at[n], cr.at[n], sib))
    lhs = rows_of(me.c)
    hr = tok // 2
    for n in range(NT):
        at = pl.ds(n * TILE, TILE)
        mine = jnp.dot(lhs, hw_ref[:, at], preferred_element_type=F32).reshape(NX, tok, TILE)
        rdma(orecv.at[n], orecv.at[n], cs.at[n], cr.at[n], sib).wait_recv()
        own[n] = mine + orecv[n].astype(F32)
        sx[n] = own[n, :3].astype(BF)
        for k, way in ((0, 1), (1, -1)):
            half = pl.ds(k * hr, hr)
            go(rdma(sx.at[n, 0, half], x1.at[k, n], xs.at[k, 0, n], xr.at[k, 0, n], me.at_x(way, me.c)))
        for k, way in ((0, 1), (1, -1)):
            half = pl.ds((1 - k) * hr, hr)
            go(rdma(sx.at[n, 1 + k, half], x2.at[k, n, half], xs.at[k, 1, n], xr.at[k, 1, n], me.at_x(way, me.c)))
    for n in range(NT):
        for k, way in ((0, 1), (1, -1)):
            blk = x1.at[k, n]
            rdma(blk, blk, xs.at[k, 0, n], xr.at[k, 0, n], me.at_x(way, me.c)).wait_recv()
            half = pl.ds(k * hr, hr)
            sx[n, 1 + k, half] = (own[n, 1 + k, half] + x1[k, n].astype(F32)).astype(BF)
            go(rdma(sx.at[n, 1 + k, half], x2.at[k, n, half], xs.at[k, 2, n], xr.at[k, 2, n], me.at_x(way, me.c)))

    tgt = jnp.broadcast_to(tgt_ref[...].astype(F32), (128, 128))
    tgt = jnp.transpose(tgt)[:tok, :1].astype(jnp.int32) - me.s * VOC
    tiles, peak = [], None
    for n in range(NT):
        for k, way in ((0, 1), (1, -1)):
            for i in range(2):
                half = pl.ds((k if i else 1 - k) * hr, hr)
                blk = x2.at[k, n, half]
                rdma(blk, blk, xs.at[k, 1 + i, n], xr.at[k, 1 + i, n], me.at_x(way, me.c)).wait_recv()
        lg = own[n, 3] + x2[0, n].astype(F32) + x2[1, n].astype(F32)
        own[n, 3] = lg
        top = jnp.max(lg, axis=1, keepdims=True)
        peak = top if peak is None else jnp.maximum(peak, top)
    total = picked = None
    for n in range(NT):
        lg = own[n, 3]
        a = jnp.sum(jnp.exp(lg - peak), axis=1, keepdims=True)
        b = jnp.sum(jnp.where(lanes((tok, TILE)) + n * TILE == tgt, lg, 0.0), axis=1, keepdims=True)
        total = a if total is None else total + a
        picked = b if picked is None else picked + b
    lane = lanes((tok, 128))
    st = jnp.where(lane == 0, peak, jnp.where(lane == 1, total, picked))
    st = jnp.concatenate([st, jnp.zeros((128 - tok, 128), F32)], axis=0)
    sty[0] = jnp.transpose(st)[:8]

    def joined(buf, count):
        top = functools.reduce(jnp.maximum, [buf[i, 0:1] for i in range(count)])
        tot = functools.reduce(jnp.add, [buf[i, 1:2] * jnp.exp(buf[i, 0:1] - top) for i in range(count)])
        pick = functools.reduce(jnp.add, [buf[i, 2:3] for i in range(count)])
        return top, tot, pick

    for d in range(1, NY):
        go(rdma(sty.at[0], sty.at[d], yss.at[d - 1], yrs.at[d - 1], me.at_y(d)))
    for d in range(1, NY):
        rdma(sty.at[d], sty.at[d], yss.at[d - 1], yrs.at[d - 1], me.at_y(d)).wait_recv()
    top, tot, pick = joined(sty, NY)
    stz[0] = jnp.concatenate([top, tot, pick, jnp.zeros((5, 128), F32)], axis=0)
    for d in range(1, NZ):
        go(rdma(stz.at[0], stz.at[d], zss.at[d - 1], zrs.at[d - 1], me.at_z(d)))
    for d in range(1, NZ):
        rdma(stz.at[d], stz.at[d], zss.at[d - 1], zrs.at[d - 1], me.at_z(d)).wait_recv()
    top, tot, pick = joined(stz, NZ)
    out_ref[...] = (pick - (top + jnp.log(tot)))[:, :tok]
    for cp in sends:
        cp.wait_send()


def vm():
    return pl.BlockSpec(memory_space=pltpu.VMEM)


def params(cid):
    return pltpu.CompilerParams(
        collective_id=cid, has_side_effects=True, vmem_limit_bytes=56 * 1024 * 1024
    )


def dma(*shape):
    return pltpu.SemaphoreType.DMA(shape)


def shards(q, sk, sv, ck, cv, start, w, res, gain, hw, tgt):
    any_ = pl.BlockSpec(memory_space=pl.ANY)
    att = pl.pallas_call(
        attention_kernel,
        out_shape=jax.ShapeDtypeStruct((ROWS, GW), BF),
        in_specs=[any_, vm(), vm(), any_, any_, pl.BlockSpec(memory_space=pltpu.SMEM)],
        out_specs=vm(),
        scratch_shapes=[
            pltpu.VMEM((NY, NZ, ROWS, GW), BF),
            pltpu.VMEM((KEYS_PAD, HS), BF),
            pltpu.VMEM((KEYS_PAD, HS), BF),
            pltpu.VMEM((KEYS_PAD, 2 * HS), BF),
            pltpu.VMEM((CACHE, 2 * HS), BF),
            pltpu.VMEM((CACHE, 2 * HS), BF),
            pltpu.VMEM((1, KEYS_PAD), F32),
            pltpu.VMEM((NZ * ROWS, 128), F32),
            pltpu.VMEM((NY, NZ, ROWS, PW), BF),
        ]
        + GATHER_SEMS
        + [dma(1), dma(2, 5), dma(NV), dma(NV), dma(2), dma(2), dma(2, 2)]
        + reduce_scratch(PW),
        compiler_params=params(0),
        name="attention",
    )(q, sk, sv, ck, cv, start)
    hidden, normed = pl.pallas_call(
        project_kernel,
        out_shape=(
            jax.ShapeDtypeStruct((ROWS, GW), BF),
            jax.ShapeDtypeStruct((NY, NZ, ROWS, GW), BF),
        ),
        in_specs=[vm()] * 4,
        out_specs=(vm(), vm()),
        scratch_shapes=[
            pltpu.VMEM((NY, ROWS, FEAT), BF),
            pltpu.VMEM((NV, NY, ROWS, FEAT), BF),
            pltpu.VMEM((NY, NZ, ROWS, GW), BF),
            pltpu.VMEM((NV, ROWS, 128), F32),
            pltpu.VMEM((NY, NZ, ROWS, GW), BF),
            dma(NY), dma(NY), dma(NV - 1), dma(NV - 1), dma(NV - 1), dma(NV - 1),
        ]
        + GATHER_SEMS
        + reduce_scratch(GW),
        compiler_params=params(1),
        name="project",
    )(att, w, res, gain.reshape(1, GW))
    tok = NY * ROWS
    logprobs = pl.pallas_call(
        logits_kernel,
        out_shape=jax.ShapeDtypeStruct((1, tok), F32),
        in_specs=[vm()] * 3,
        out_specs=vm(),
        scratch_shapes=[
            pltpu.VMEM((NT, NX, tok, TILE), BF),
            pltpu.VMEM((NT, NX, tok, TILE), BF),
            pltpu.VMEM((NT, NX, tok, TILE), F32),
            pltpu.VMEM((NT, 3, tok, TILE), BF),
            pltpu.VMEM((2, NT, tok // 2, TILE), BF),
            pltpu.VMEM((2, NT, tok, TILE), BF),
            pltpu.VMEM((NY, 8, 128), F32),
            pltpu.VMEM((NZ, 8, 128), F32),
            dma(NT), dma(NT), dma(2, 3, NT), dma(2, 3, NT),
            dma(NY - 1), dma(NY - 1), dma(NZ - 1), dma(NZ - 1),
        ],
        compiler_params=params(2),
        name="logits",
    )(normed, hw, jnp.pad(tgt.reshape(1, tok), ((0, 0), (0, 128 - tok))))
    return hidden, logprobs.reshape(tok)


def solution(mesh):
    placed = (
        P("seq", None),
        P("seq", None),
        P("seq", None),
        P(("seq", "vocab"), None),
        P(("seq", "vocab"), None),
        P(),
        P("seq", "vocab"),
        P("seq", "vocab"),
        P("vocab"),
        P("vocab", "seq"),
        P("vocab"),
    )
    return jax.shard_map(
        shards,
        mesh=mesh,
        in_specs=placed,
        out_specs=(P("seq", "vocab"), P("vocab")),
        check_vma=False,
    )
```

```python
import functools
import math

import jax
import jax.numpy as jnp
from jax import lax
from jax.experimental import pallas as pl
from jax.experimental.pallas import tpu as pltpu
from jax.sharding import PartitionSpec as P

D = 8192
HEADS = 8
HS = 128
NY, NZ, NX = 4, 8, 4
NV = 2 * NX
ROWS = 16
CACHE = 256
KEYS = NV * CACHE
KEYS_PAD = KEYS + 128
GW = HEADS * HS
PW = GW + 128
VOC = 2048
TILE = 512
NT = VOC // TILE
FEAT = 256
BIG_NEG = -1e30
EPSILON = 1e-05
MESH = pl.DeviceIdType.MESH
BF = jnp.bfloat16
F32 = jnp.float32


class Place:
    def __init__(self):
        s, v = lax.axis_index("seq"), lax.axis_index("vocab")
        self.s, self.v = s, v
        self.z, self.y = lax.div(s, NY), lax.rem(s, NY)
        self.x, self.c = lax.div(v, 2), lax.rem(v, 2)

    def yy(self, d):
        return lax.rem(self.y + d + NY, NY)

    def zz(self, d):
        return lax.rem(self.z + d + NZ, NZ)

    def xx(self, d):
        return lax.rem(self.x + d + NX, NX)

    def at_z(self, d):
        return (self.zz(d) * NY + self.y, self.v)

    def at_y(self, d):
        return (self.z * NY + self.yy(d), self.v)

    def at_x(self, d, core):
        return (self.s, self.xx(d) * 2 + core)

    def at_v(self, d):
        return (self.s, lax.rem(self.v + d, NV))


def rdma(src, dst, send, recv, dev):
    return pltpu.make_async_remote_copy(
        src_ref=src, dst_ref=dst, send_sem=send, recv_sem=recv, device_id=dev, device_id_type=MESH
    )


def greet(partners):
    bar = pltpu.get_barrier_semaphore()
    for dev in partners:
        pl.semaphore_signal(bar, inc=1, device_id=dev, device_id_type=MESH)
    pl.semaphore_wait(bar, len(partners))


def gather_start(me, go, buf, zs, zr):
    own = buf.at[me.y, me.z]
    for d in (1, 7, 2, 6, 3, 5, 4):
        go(rdma(own, own, zs.at[d - 1], zr.at[d - 1], me.at_z(d)))


def gather_seq(me, go, buf, zs, zr, ys, yr):
    for d in (0, 1, 7, 2, 6, 3, 5, 4):
        blk = buf.at[me.y, me.zz(-d)]
        if d:
            rdma(blk, blk, zs.at[d - 1], zr.at[d - 1], me.at_z(1)).wait_recv()
        for e in (2, 1, 3):
            go(rdma(blk, blk, ys.at[e - 1, d], yr.at[e - 1, d], me.at_y(e)))


def gather_wait(me, buf, ys, yr):
    for e in (2, 1, 3):
        for d in range(NZ):
            blk = buf.at[me.yy(-e), me.zz(-d)]
            rdma(blk, blk, ys.at[e - 1, d], yr.at[e - 1, d], me.at_y(e)).wait_recv()


def ring_step(me, go, step, buf, ss, rs):
    rows = buf.shape[1]
    for k, way in ((0, 1), (1, -1)):
        if step == 1:
            blk = buf.at[me.z]
        else:
            blk = buf.at[me.zz(-way * (step - 1))]
            rdma(blk, blk, ss.at[k, step - 2], rs.at[k, step - 2], me.at_z(way)).wait_recv()
        if step == NZ // 2:
            blk = buf.at[me.zz(-way * (step - 1)), pl.ds(k * (rows // 2), rows // 2)]
        go(rdma(blk, blk, ss.at[k, step - 1], rs.at[k, step - 1], me.at_z(way)))


def ring_wait(me, buf, ss, rs):
    rows = buf.shape[1]
    step = NZ // 2
    for k, way in ((0, 1), (1, -1)):
        blk = buf.at[me.zz(step), pl.ds(k * (rows // 2), rows // 2)]
        rdma(blk, blk, ss.at[k, step - 1], rs.at[k, step - 1], me.at_z(way)).wait_recv()


def lanes(shape):
    return lax.broadcasted_iota(jnp.int32, shape, len(shape) - 1)


def pack_lse(lse, low8):
    second = pltpu.roll(lse, 8, 1) if low8 else lse
    third = pltpu.roll(lse, 16, 1) if low8 else lse

    def split(a):
        hi = a.astype(BF).astype(F32)
        mid = (a - hi).astype(BF).astype(F32)
        return hi, mid, a - hi - mid

    lane = lanes(lse.shape)
    out = jnp.where(lane < 8, split(lse)[0], jnp.where(lane < 16, split(second)[1], split(third)[2]))
    return jnp.where(lane < 24, out, 0.0).astype(BF)


def unpack_lse(packed):
    a = packed.astype(F32)
    return a + (pltpu.roll(a, 120, 1) + pltpu.roll(a, 112, 1))


def join_partials(items, final=False):
    lses = [unpack_lse(it[:, GW:]) for it in items]
    peak = functools.reduce(jnp.maximum, lses)
    weights = [jnp.exp2(l - peak) for l in lses]
    total = functools.reduce(jnp.add, weights)
    weights = [w / total for w in weights]
    cols = []
    for h in range(HEADS):
        acc = None
        for w, it in zip(weights, items):
            term = w[:, h : h + 1] * it[:, h * HS : (h + 1) * HS].astype(F32)
            acc = term if acc is None else acc + term
        cols.append(acc.astype(BF))
    if not final:
        cols.append(pack_lse(peak + jnp.log2(total), True))
    return jnp.concatenate(cols, axis=1)


def kernel(
    q_ref, sk_ref, sv_ref, ck_ref, cv_ref, start_ref, w_ref, res_ref, gain_ref, hw_hbm, tgt_ref,
    hid_ref, out_ref,
    qall, kbuf, vbuf, vext, bias, lse_buf, opart, ry, mg, rz, wall, hw_ref, tin, aall, ppart, rp, sq, nall,
    osend, orecv, own, sx, x2, sty, stz,
    loc, kvs, kr, vr, gz, gzr, gy, gyr, ws, wr, rys, ryr, rzs, rzr, tss, trs, avs, avr, ps_, pr_, sqs, sqr,
    hz, hzr, hy, hyr, cs, cr, xs, xr, yss, yrs, zss, zrs,
):
    me = Place()
    sends = []

    def go(cp):
        cp.start()
        sends.append(cp)

    def cols(vv):
        return pl.ds(pl.multiple_of(vv * HS, HS), HS)

    def rows(vv):
        return pl.ds(pl.multiple_of(vv * CACHE, CACHE), CACHE)

    head_cols = pl.ds(pl.multiple_of(me.v * GW, GW), GW)
    own_q = pltpu.make_async_copy(q_ref.at[:, head_cols], qall.at[me.y, me.z], loc.at[0])
    own_q.start()
    own_w = pltpu.make_async_copy(w_ref, wall.at[me.z], loc.at[1])
    own_w.start()
    own_k = pltpu.make_async_copy(ck_ref.at[:, cols(me.v)], kbuf.at[rows(me.v)], kr.at[me.v])
    own_v = pltpu.make_async_copy(cv_ref.at[:, cols(me.v)], vbuf.at[rows(me.v)], vr.at[me.v])
    own_k.start()
    own_v.start()
    own_hw = pltpu.make_async_copy(hw_hbm, hw_ref, loc.at[2])
    own_hw.start()
    kbuf[KEYS:, :] = jnp.zeros((128, HS), BF)
    vbuf[KEYS:, :] = jnp.zeros((128, HS), BF)
    kbuf[KEYS : KEYS + ROWS, :] = sk_ref[:, cols(me.v)]
    vbuf[KEYS : KEYS + ROWS, :] = sv_ref[:, cols(me.v)]
    flat = lanes((1, KEYS_PAD))
    bias[...] = jnp.where(flat < start_ref[0] - me.s * KEYS, 0.0, BIG_NEG)
    own_q.wait()
    greet(
        [me.at_z(d) for d in range(1, NZ)]
        + [me.at_y(d) for d in range(1, NY)]
        + [me.at_v(d) for d in range(1, NV)]
    )

    gather_start(me, go, qall, gz, gzr)
    for i, d in enumerate((4, 3, 5, 2, 6, 1, 7)):
        vv = lax.rem(me.v + d, NV)
        go(rdma(ck_ref.at[:, cols(vv)], kbuf.at[rows(me.v)], kvs.at[0, i], kr.at[me.v], me.at_v(d)))
        go(rdma(cv_ref.at[:, cols(vv)], vbuf.at[rows(me.v)], kvs.at[1, i], vr.at[me.v], me.at_v(d)))
    gather_seq(me, go, qall, gz, gzr, gy, gyr)
    own_w.wait()
    ring_step(me, go, 1, wall, ws, wr)
    own_k.wait()
    own_v.wait()
    for d in range(1, NV):
        src = lax.rem(me.v + d, NV)
        blk = kbuf.at[rows(src)]
        rdma(blk, blk, kvs.at[0, 0], kr.at[src], me.at_v(1)).wait_recv()
        blk = vbuf.at[rows(src)]
        rdma(blk, blk, kvs.at[1, 0], vr.at[src], me.at_v(1)).wait_recv()
    vext[:, :HS] = vbuf[...]
    vext[:, HS:] = jnp.ones((KEYS_PAD, HS), BF)
    gather_wait(me, qall, gy, gyr)

    scale = math.log2(math.e) / math.sqrt(HS)
    nrow = NZ * ROWS
    for turn, order in enumerate((2, 1, 3, 0)):
        yy = me.yy(order)
        if turn:
            ring_step(me, go, turn + 1, wall, ws, wr)

        def pair(hp, carry):
            both = []
            for i in range(2):
                at = pl.ds(pl.multiple_of((hp * 2 + i) * HS, HS), HS)
                both.append(qall[yy, :, :, at].reshape(nrow, HS))
            q2 = jnp.concatenate(both, axis=0)
            sc = lax.dot_general(q2, kbuf[...], (((1,), (1,)), ((), ())), preferred_element_type=F32)
            main = sc[:, :KEYS] * scale + bias[:, :KEYS]
            row = lax.broadcasted_iota(jnp.int32, (2 * nrow, 128), 0)
            row = lax.rem(row, nrow)
            token = lax.div(row, ROWS) * (NY * ROWS) + yy * ROWS + lax.rem(row, ROWS)
            key = lanes((2 * nrow, 128))
            ok = (key < ROWS) & (key + me.s * ROWS <= token)
            span = jnp.where(ok, sc[:, KEYS:] * scale, BIG_NEG)
            peak = jnp.maximum(
                jnp.max(main, axis=1, keepdims=True), jnp.max(span, axis=1, keepdims=True)
            )
            pm = jnp.exp2(main - peak).astype(BF)
            ps = jnp.exp2(span - peak).astype(BF)
            ps = jnp.where(ok, ps, jnp.zeros_like(ps))
            o = jnp.dot(pm, vext[:KEYS, :], preferred_element_type=F32)
            o = o + jnp.dot(ps, vext[KEYS:, :], preferred_element_type=F32)
            total = o[:, HS:]
            total = jnp.where(total > 0.0, total, 1.0)
            on = (o[:, :HS] / total).astype(BF)
            lse = peak + jnp.log2(total)
            lane = lanes((nrow, 128))
            for i in range(2):
                h = hp * 2 + i
                at = pl.ds(pl.multiple_of(h * HS, HS), HS)
                opart[yy, :, :, at] = on[i * nrow : (i + 1) * nrow].reshape(NZ, ROWS, HS)
                mine = lse[i * nrow : (i + 1) * nrow]
                lse_buf[...] = jnp.where(lax.rem(lane, 8) == h, mine, lse_buf[...])
            return carry

        lax.fori_loop(0, HEADS // 2, pair, 0)
        opart[yy, :, :, GW:] = pack_lse(lse_buf[...], False).reshape(NZ, ROWS, 128)
        if order:
            go(rdma(opart.at[yy], ry.at[order - 1], rys.at[order - 1], ryr.at[order - 1], me.at_y(order)))

    items = [opart[me.y].reshape(nrow, PW)]
    for d in (2, 1, 3):
        blk = ry.at[d - 1]
        rdma(blk, blk, rys.at[d - 1], ryr.at[d - 1], me.at_y(d)).wait_recv()
        items.append(ry[d - 1].reshape(nrow, PW))
    mg[...] = join_partials(items).reshape(NZ, ROWS, PW)
    for d in (4, 3, 5, 2, 6, 1, 7):
        go(rdma(mg.at[me.zz(d)], rz.at[d - 1], rzs.at[d - 1], rzr.at[d - 1], me.at_z(d)))
    items = [mg[me.z]]
    for d in range(1, NZ):
        blk = rz.at[d - 1]
        rdma(blk, blk, rzs.at[d - 1], rzr.at[d - 1], me.at_z(d)).wait_recv()
        items.append(rz[d - 1])
    att = join_partials(items, final=True)

    for j in range(NY):
        tin[0, j] = att[:, j * FEAT : (j + 1) * FEAT]
    aall[me.v, me.y] = tin[0, me.y]
    for d in (2, 1, 3):
        go(rdma(tin.at[0, me.yy(d)], aall.at[me.v, me.y], tss.at[d - 1], trs.at[d - 1], me.at_y(d)))
    for d in (2, 1, 3):
        blk = aall.at[me.v, me.yy(-d)]
        rdma(blk, blk, tss.at[d - 1], trs.at[d - 1], me.at_y(d)).wait_recv()
    for d in (4, 3, 5, 2, 6, 1, 7):
        blk = aall.at[me.v]
        go(rdma(blk, blk, avs.at[d - 1], avr.at[d - 1], me.at_v(d)))
    ring_wait(me, wall, ws, wr)
    tok = NY * ROWS
    proj = jnp.dot(aall[me.v].reshape(tok, FEAT), wall[me.v], preferred_element_type=F32)
    for d in (1, 7, 2, 6, 3, 5, 4):
        src = lax.rem(me.v - d + NV, NV)
        blk = aall.at[src]
        rdma(blk, blk, avs.at[d - 1], avr.at[d - 1], me.at_v(1)).wait_recv()
        proj = proj + jnp.dot(aall[src].reshape(tok, FEAT), wall[src], preferred_element_type=F32)
    ppart[...] = proj.astype(BF).reshape(NY, ROWS, GW)
    for d in (2, 1, 3):
        go(rdma(ppart.at[me.yy(d)], rp.at[d - 1], ps_.at[d - 1], pr_.at[d - 1], me.at_y(d)))
    total = res_ref[...].astype(F32) + ppart[me.y].astype(F32)
    for d in (1, 3, 2):
        blk = rp.at[d - 1]
        rdma(blk, blk, ps_.at[d - 1], pr_.at[d - 1], me.at_y(d)).wait_recv()
        total = total + rp[d - 1].astype(F32)
    hidden = total.astype(BF)
    hid_ref[...] = hidden

    wide = hidden.astype(F32)
    sq[me.v] = jnp.broadcast_to(jnp.sum(wide * wide, axis=1, keepdims=True), (ROWS, 128))
    for d in (4, 3, 5, 2, 6, 1, 7):
        go(rdma(sq.at[me.v], sq.at[me.v], sqs.at[d - 1], sqr.at[d - 1], me.at_v(d)))
    for d in range(1, NV):
        blk = sq.at[lax.rem(me.v - d + NV, NV)]
        rdma(blk, blk, sqs.at[d - 1], sqr.at[d - 1], me.at_v(1)).wait_recv()
    mean = jnp.sum(sq[...], axis=0)[:, :1] * (1.0 / D)
    nall[me.y, me.z] = (wide * lax.rsqrt(mean + EPSILON) * gain_ref[...]).astype(BF)
    gather_start(me, go, nall, hz, hzr)
    gather_seq(me, go, nall, hz, hzr, hy, hyr)
    own_hw.wait()
    gather_wait(me, nall, hy, hyr)

    shift = (2, 1, 3, 0)

    def rows_of(core):
        blocks = []
        for d in shift:
            for y in range(NY):
                blocks.append(nall[y, me.xx(d) * 2 + core])
        return jnp.concatenate(blocks, axis=0)

    sib = me.at_x(0, 1 - me.c)
    lhs = rows_of(1 - me.c)
    for n in range(NT):
        at = pl.ds(n * TILE, TILE)
        osend[n] = (
            jnp.dot(lhs, hw_ref[:, at], preferred_element_type=F32).astype(BF).reshape(NX, tok, TILE)
        )
        go(rdma(osend.at[n], orecv.at[n], cs.at[n], cr.at[n], sib))
    lhs = rows_of(me.c)
    for n in range(NT):
        at = pl.ds(n * TILE, TILE)
        mine = jnp.dot(lhs, hw_ref[:, at], preferred_element_type=F32).reshape(NX, tok, TILE)
        rdma(orecv.at[n], orecv.at[n], cs.at[n], cr.at[n], sib).wait_recv()
        mine = mine + orecv[n].astype(F32)
        own[n] = mine[3]
        sx[n] = mine[:3].astype(BF)
        for i, d in enumerate(shift[:3]):
            go(rdma(sx.at[n, i], x2.at[n, i], xs.at[n, i], xr.at[n, i], me.at_x(d, me.c)))

    tgt = jnp.concatenate([tgt_ref[...], jnp.zeros((1, 128 - tok), jnp.int32)], axis=1)
    tgt = jnp.broadcast_to(tgt.astype(F32), (128, 128))
    tgt = jnp.transpose(tgt)[:tok, :1].astype(jnp.int32) - me.s * VOC
    peak = None
    for n in range(NT):
        lg = own[n]
        for i, d in enumerate(shift[:3]):
            blk = x2.at[n, i]
            rdma(blk, blk, xs.at[n, i], xr.at[n, i], me.at_x(d, me.c)).wait_recv()
            lg = lg + x2[n, i].astype(F32)
        own[n] = lg
        top = jnp.max(lg, axis=1, keepdims=True)
        peak = top if peak is None else jnp.maximum(peak, top)
    total = picked = None
    for n in range(NT):
        lg = own[n]
        a = jnp.sum(jnp.exp(lg - peak), axis=1, keepdims=True)
        b = jnp.sum(jnp.where(lanes((tok, TILE)) + n * TILE == tgt, lg, 0.0), axis=1, keepdims=True)
        total = a if total is None else total + a
        picked = b if picked is None else picked + b
    lane = lanes((tok, 128))
    st = jnp.where(lane == 0, peak, jnp.where(lane == 1, total, picked))
    st = jnp.concatenate([st, jnp.zeros((128 - tok, 128), F32)], axis=0)
    sty[0] = jnp.transpose(st)[:8]

    def joined(buf, count):
        top = functools.reduce(jnp.maximum, [buf[i, 0:1] for i in range(count)])
        tot = functools.reduce(jnp.add, [buf[i, 1:2] * jnp.exp(buf[i, 0:1] - top) for i in range(count)])
        pick = functools.reduce(jnp.add, [buf[i, 2:3] for i in range(count)])
        return top, tot, pick

    for d in (2, 1, 3):
        go(rdma(sty.at[0], sty.at[d], yss.at[d - 1], yrs.at[d - 1], me.at_y(d)))
    for d in range(1, NY):
        rdma(sty.at[d], sty.at[d], yss.at[d - 1], yrs.at[d - 1], me.at_y(d)).wait_recv()
    top, tot, pick = joined(sty, NY)
    stz[0] = jnp.concatenate([top, tot, pick, jnp.zeros((5, 128), F32)], axis=0)
    for d in (4, 3, 5, 2, 6, 1, 7):
        go(rdma(stz.at[0], stz.at[d], zss.at[d - 1], zrs.at[d - 1], me.at_z(d)))
    for d in range(1, NZ):
        rdma(stz.at[d], stz.at[d], zss.at[d - 1], zrs.at[d - 1], me.at_z(d)).wait_recv()
    top, tot, pick = joined(stz, NZ)
    out_ref[...] = (pick - (top + jnp.log(tot)))[:, :tok]
    for cp in sends:
        cp.wait_send()


def vm():
    return pl.BlockSpec(memory_space=pltpu.VMEM)


def params(cid):
    return pltpu.CompilerParams(
        collective_id=cid, has_side_effects=True, vmem_limit_bytes=56 * 1024 * 1024
    )


def dma(*shape):
    return pltpu.SemaphoreType.DMA(shape)


def shards(q, sk, sv, ck, cv, start, w, res, gain, hw, tgt):
    any_ = pl.BlockSpec(memory_space=pl.ANY)
    tok = NY * ROWS
    hidden, logprobs = pl.pallas_call(
        kernel,
        out_shape=(
            jax.ShapeDtypeStruct((ROWS, GW), BF),
            jax.ShapeDtypeStruct((1, tok), F32),
        ),
        in_specs=[any_, vm(), vm(), any_, any_, pl.BlockSpec(memory_space=pltpu.SMEM)]
        + [any_, vm(), vm(), any_, vm()],
        out_specs=(vm(), vm()),
        scratch_shapes=[
            pltpu.VMEM((NY, NZ, ROWS, GW), BF),
            pltpu.VMEM((KEYS_PAD, HS), BF),
            pltpu.VMEM((KEYS_PAD, HS), BF),
            pltpu.VMEM((KEYS_PAD, 2 * HS), BF),
            pltpu.VMEM((1, KEYS_PAD), F32),
            pltpu.VMEM((NZ * ROWS, 128), F32),
            pltpu.VMEM((NY, NZ, ROWS, PW), BF),
            pltpu.VMEM((NY - 1, NZ, ROWS, PW), BF),
            pltpu.VMEM((NZ, ROWS, PW), BF),
            pltpu.VMEM((NZ - 1, ROWS, PW), BF),
            pltpu.VMEM((NZ, FEAT, GW), BF),
            pltpu.VMEM((GW, VOC), BF),
            pltpu.VMEM((1, NY, ROWS, FEAT), BF),
            pltpu.VMEM((NV, NY, ROWS, FEAT), BF),
            pltpu.VMEM((NY, ROWS, GW), BF),
            pltpu.VMEM((NY - 1, ROWS, GW), BF),
            pltpu.VMEM((NV, ROWS, 128), F32),
            pltpu.VMEM((NY, NZ, ROWS, GW), BF),
            pltpu.VMEM((NT, NX, tok, TILE), BF),
            pltpu.VMEM((NT, NX, tok, TILE), BF),
            pltpu.VMEM((NT, tok, TILE), F32),
            pltpu.VMEM((NT, NX - 1, tok, TILE), BF),
            pltpu.VMEM((NT, NX - 1, tok, TILE), BF),
            pltpu.VMEM((NY, 8, 128), F32),
            pltpu.VMEM((NZ, 8, 128), F32),
            dma(3), dma(2, NV - 1), dma(NV), dma(NV),
            dma(NZ - 1), dma(NZ - 1), dma(NY - 1, NZ), dma(NY - 1, NZ),
            dma(2, NZ // 2), dma(2, NZ // 2),
            dma(NY - 1), dma(NY - 1), dma(NZ - 1), dma(NZ - 1),
            dma(NY - 1), dma(NY - 1), dma(NV - 1), dma(NV - 1),
            dma(NY - 1), dma(NY - 1), dma(NV - 1), dma(NV - 1),
            dma(NZ - 1), dma(NZ - 1), dma(NY - 1, NZ), dma(NY - 1, NZ),
            dma(NT), dma(NT), dma(NT, NX - 1), dma(NT, NX - 1),
            dma(NY - 1), dma(NY - 1), dma(NZ - 1), dma(NZ - 1),
        ],
        compiler_params=params(0),
        name="layer",
    )(q, sk, sv, ck, cv, start, w, res, gain.reshape(1, GW), hw, tgt.reshape(1, tok))
    return hidden, logprobs.reshape(tok)


def solution(mesh):
    placed = (
        P("seq", None),
        P("seq", None),
        P("seq", None),
        P(("seq", "vocab"), None),
        P(("seq", "vocab"), None),
        P(),
        P("seq", "vocab"),
        P("seq", "vocab"),
        P("vocab"),
        P("vocab", "seq"),
        P("vocab"),
    )
    return jax.shard_map(
        shards,
        mesh=mesh,
        in_specs=placed,
        out_specs=(P("seq", "vocab"), P("vocab")),
        check_vma=False,
    )
```

```python
import functools
import math

import jax
import jax.numpy as jnp
from jax import lax
from jax.experimental import pallas as pl
from jax.experimental.pallas import tpu as pltpu
from jax.sharding import PartitionSpec as P

D = 8192
HEADS = 8
HS = 128
NY, NZ, NX = 4, 8, 4
NV = 2 * NX
ROWS = 16
CACHE = 256
KEYS = NV * CACHE
KEYS_PAD = KEYS + 128
GW = HEADS * HS
PW = GW + 128
VOC = 2048
TILE = 512
NT = VOC // TILE
FEAT = 256
BIG_NEG = -1e30
EPSILON = 1e-05
MESH = pl.DeviceIdType.MESH
BF = jnp.bfloat16
F32 = jnp.float32


class Place:
    def __init__(self):
        s, v = lax.axis_index("seq"), lax.axis_index("vocab")
        self.s, self.v = s, v
        self.z, self.y = lax.div(s, NY), lax.rem(s, NY)
        self.x, self.c = lax.div(v, 2), lax.rem(v, 2)

    def yy(self, d):
        return lax.rem(self.y + d + NY, NY)

    def zz(self, d):
        return lax.rem(self.z + d + NZ, NZ)

    def xx(self, d):
        return lax.rem(self.x + d + NX, NX)

    def at_z(self, d):
        return (self.zz(d) * NY + self.y, self.v)

    def at_y(self, d):
        return (self.z * NY + self.yy(d), self.v)

    def at_x(self, d, core):
        return (self.s, self.xx(d) * 2 + core)

    def at_v(self, d):
        return (self.s, lax.rem(self.v + d, NV))


def rdma(src, dst, send, recv, dev):
    return pltpu.make_async_remote_copy(
        src_ref=src, dst_ref=dst, send_sem=send, recv_sem=recv, device_id=dev, device_id_type=MESH
    )


def greet(partners):
    bar = pltpu.get_barrier_semaphore()
    for dev in partners:
        pl.semaphore_signal(bar, inc=1, device_id=dev, device_id_type=MESH)


def gather_start(me, go, buf, zs, zr):
    own = buf.at[me.y, me.z]
    for d in (1, 7, 2, 6, 3, 5, 4):
        go(rdma(own, own, zs.at[d - 1], zr.at[me.z], me.at_z(d)))


def gather_pass(me, go, buf, src, own, zs, zr, ys, yr):
    blk = buf.at[me.y, src]
    if not own:
        rdma(blk, blk, zs.at[0], zr.at[src], me.at_z(1)).wait_recv()
    for e in (2, 1, 3):
        go(rdma(blk, blk, ys.at[e - 1, src], yr.at[e - 1, src], me.at_y(e)))


def gather_wait(me, buf, e, src, ys, yr):
    blk = buf.at[me.yy(-e), src]
    rdma(blk, blk, ys.at[e - 1, src], yr.at[e - 1, src], me.at_y(e)).wait_recv()


PIECES = 4
TICKS = [(step, p) for step in range(NZ // 2 - 1) for p in range(PIECES)]
TICKS += [(NZ // 2 - 1, p) for p in range(PIECES // 2)]


def ring_piece(me, buf, k, way, step, p):
    rows = buf.shape[1] // PIECES
    p = p + k * (PIECES // 2) if step == NZ // 2 - 1 else p
    return buf.at[me.zz(-way * step), pl.ds(p * rows, rows)], p


def ring_tick(me, go, tick, buf, ss, rs):
    step, p0 = TICKS[tick]
    for k, way in ((0, 1), (1, -1)):
        blk, p = ring_piece(me, buf, k, way, step, p0)
        if step:
            rdma(blk, blk, ss.at[k, 0], rs.at[k, (step - 1) * PIECES + p], me.at_z(way)).wait_recv()
        go(rdma(blk, blk, ss.at[k, tick], rs.at[k, step * PIECES + p], me.at_z(way)))


def ring_wait(me, buf, ss, rs):
    last = NZ // 2 - 1
    rows = buf.shape[1] // PIECES
    for k, way in ((0, 1), (1, -1)):
        for p in range(PIECES):
            if p // (PIECES // 2) == k:
                blk = buf.at[me.zz(-way * (last + 1)), pl.ds(p * rows, rows)]
                rdma(blk, blk, ss.at[k, 0], rs.at[k, last * PIECES + p], me.at_z(way)).wait_recv()
            else:
                blk = buf.at[me.zz(-way * last), pl.ds(p * rows, rows)]
                rdma(blk, blk, ss.at[k, 0], rs.at[k, (last - 1) * PIECES + p], me.at_z(way)).wait_recv()


def lanes(shape):
    return lax.broadcasted_iota(jnp.int32, shape, len(shape) - 1)


def pack_lse(lse, low8):
    second = pltpu.roll(lse, 8, 1) if low8 else lse
    third = pltpu.roll(lse, 16, 1) if low8 else lse

    def split(a):
        hi = a.astype(BF).astype(F32)
        mid = (a - hi).astype(BF).astype(F32)
        return hi, mid, a - hi - mid

    lane = lanes(lse.shape)
    out = jnp.where(lane < 8, split(lse)[0], jnp.where(lane < 16, split(second)[1], split(third)[2]))
    return jnp.where(lane < 24, out, 0.0).astype(BF)


def unpack_lse(packed):
    a = packed.astype(F32)
    return a + (pltpu.roll(a, 120, 1) + pltpu.roll(a, 112, 1))


def join_partials(items, final=False):
    lses = [unpack_lse(it[:, GW:]) for it in items]
    peak = functools.reduce(jnp.maximum, lses)
    weights = [jnp.exp2(l - peak) for l in lses]
    total = functools.reduce(jnp.add, weights)
    weights = [w / total for w in weights]
    cols = []
    for h in range(HEADS):
        acc = None
        for w, it in zip(weights, items):
            term = w[:, h : h + 1] * it[:, h * HS : (h + 1) * HS].astype(F32)
            acc = term if acc is None else acc + term
        cols.append(acc.astype(BF))
    if not final:
        cols.append(pack_lse(peak + jnp.log2(total), True))
    return jnp.concatenate(cols, axis=1)


def kernel(
    q_ref, sk_ref, sv_ref, ck_ref, cv_ref, start_ref, w_ref, res_hbm, gain_hbm, hw_hbm, tgt_hbm,
    hid_ref, out_ref,
    qall, kbuf, vbuf, vext, bias, lse_buf, opart, ry, mg, rz, wall, hw_ref, res_ref, gain_ref, tgt_ref, tin, aall, ppart, rp, sq, nall,
    osend, orecv, own, final, sx, x2, sty, stz,
    loc, kvs, kr, vr, gz, gzr, gy, gyr, ws, wr, rys, ryr, rzs, rzr, avs, avr, ps_, pr_, sqs, sqr,
    hz, hzr, hy, hyr, cs, cr, xs, xr, yss, yrs, zss, zrs,
):
    me = Place()
    sends = []

    def go(cp):
        cp.start()
        sends.append(cp)

    def cols(vv):
        return pl.ds(pl.multiple_of(vv * HS, HS), HS)

    def rows(vv):
        return pl.ds(pl.multiple_of(vv * CACHE, CACHE), CACHE)

    greet(
        [me.at_z(d) for d in range(1, NZ)]
        + [
            (me.z * NY + me.yy(dy), lax.rem(me.v + dv, NV))
            for dy in range(NY)
            for dv in range(NV)
            if dy or dv
        ]
    )

    def fetch(src, dst, sem):
        cp = pltpu.make_async_copy(src, dst, sem)
        cp.start()
        return cp

    head_cols = pl.ds(pl.multiple_of(me.v * GW, GW), GW)
    own_q = fetch(q_ref.at[:, head_cols], qall.at[me.y, me.z], loc.at[0])
    own_w = fetch(w_ref, wall.at[me.z], loc.at[1])
    own_k = fetch(ck_ref.at[:, cols(me.v)], kbuf.at[rows(me.v)], kr.at[me.v])
    own_v = fetch(cv_ref.at[:, cols(me.v)], vbuf.at[rows(me.v)], vr.at[me.v])
    span_k = fetch(sk_ref.at[:, cols(me.v)], kbuf.at[pl.ds(KEYS, ROWS)], loc.at[3])
    span_v = fetch(sv_ref.at[:, cols(me.v)], vbuf.at[pl.ds(KEYS, ROWS)], loc.at[4])
    later = [fetch(hw_hbm, hw_ref, loc.at[2]), fetch(res_hbm, res_ref, loc.at[5])]
    later += [fetch(gain_hbm, gain_ref, loc.at[6]), fetch(tgt_hbm, tgt_ref, loc.at[7])]
    kbuf[KEYS + ROWS :, :] = jnp.zeros((128 - ROWS, HS), BF)
    vbuf[KEYS + ROWS :, :] = jnp.zeros((128 - ROWS, HS), BF)
    flat = lanes((1, KEYS_PAD))
    bias[...] = jnp.where(flat < start_ref[0] - me.s * KEYS, 0.0, BIG_NEG)
    own_q.wait()
    own_w.wait()
    pl.semaphore_wait(pltpu.get_barrier_semaphore(), NZ - 1 + NY * NV - 1)

    gather_start(me, go, qall, gz, gzr)
    for i, d in enumerate((4, 3, 5, 2, 6, 1, 7)):
        vv = lax.rem(me.v + d, NV)
        go(rdma(ck_ref.at[:, cols(vv)], kbuf.at[rows(me.v)], kvs.at[0, i], kr.at[me.v], me.at_v(d)))
        go(rdma(cv_ref.at[:, cols(vv)], vbuf.at[rows(me.v)], kvs.at[1, i], vr.at[me.v], me.at_v(d)))
    ring_tick(me, go, 0, wall, ws, wr)
    ring_tick(me, go, 1, wall, ws, wr)
    for d in (0, 1, 7, 2, 6, 3, 5, 4):
        gather_pass(me, go, qall, me.zz(d), d == 0, gz, gzr, gy, gyr)
    ring_tick(me, go, 2, wall, ws, wr)
    ring_tick(me, go, 3, wall, ws, wr)
    span_k.wait()
    span_v.wait()
    own_k.wait()
    own_v.wait()
    for d in range(1, NV):
        src = lax.rem(me.v + d, NV)
        blk = kbuf.at[rows(src)]
        rdma(blk, blk, kvs.at[0, 0], kr.at[src], me.at_v(1)).wait_recv()
        blk = vbuf.at[rows(src)]
        rdma(blk, blk, kvs.at[1, 0], vr.at[src], me.at_v(1)).wait_recv()
    vext[:, :HS] = vbuf[...]
    vext[:, HS:] = jnp.ones((KEYS_PAD, HS), BF)
    ring_tick(me, go, 4, wall, ws, wr)

    scale = math.log2(math.e) / math.sqrt(HS)
    nrow = NZ * ROWS
    for turn, order in enumerate((2, 1, 3, 0)):
        yy = me.yy(order)
        if order:
            for d in (0, 1, 7, 2, 6, 3, 5, 4):
                gather_wait(me, qall, NY - order, me.zz(d), gy, gyr)

        def pair(hp):
            both = []
            for i in range(2):
                at = pl.ds((hp * 2 + i) * HS, HS)
                both.append(qall[yy, :, :, at].reshape(nrow, HS))
            q2 = jnp.concatenate(both, axis=0)
            sc = lax.dot_general(q2, kbuf[...], (((1,), (1,)), ((), ())), preferred_element_type=F32)
            main = sc[:, :KEYS] * scale + bias[:, :KEYS]
            row = lax.broadcasted_iota(jnp.int32, (2 * nrow, 128), 0)
            row = lax.rem(row, nrow)
            token = lax.div(row, ROWS) * (NY * ROWS) + yy * ROWS + lax.rem(row, ROWS)
            key = lanes((2 * nrow, 128))
            ok = (key < ROWS) & (key + me.s * ROWS <= token)
            span = jnp.where(ok, sc[:, KEYS:] * scale, BIG_NEG)
            peak = jnp.maximum(
                jnp.max(main, axis=1, keepdims=True), jnp.max(span, axis=1, keepdims=True)
            )
            pm = jnp.exp2(main - peak).astype(BF)
            ps = jnp.exp2(span - peak).astype(BF)
            ps = jnp.where(ok, ps, jnp.zeros_like(ps))
            o = jnp.dot(pm, vext[:KEYS, :], preferred_element_type=F32)
            o = o + jnp.dot(ps, vext[KEYS:, :], preferred_element_type=F32)
            total = o[:, HS:]
            total = jnp.where(total > 0.0, total, 1.0)
            on = (o[:, :HS] / total).astype(BF)
            lse = peak + jnp.log2(total)
            lane = lanes((nrow, 128))
            for i in range(2):
                h = hp * 2 + i
                at = pl.ds(h * HS, HS)
                opart[yy, :, :, at] = on[i * nrow : (i + 1) * nrow].reshape(NZ, ROWS, HS)
                mine = lse[i * nrow : (i + 1) * nrow]
                lse_buf[...] = jnp.where(lax.rem(lane, 8) == h, mine, lse_buf[...])

        def ship(part):
            at = pl.ds(0, GW // 2) if part == 0 else pl.ds(GW // 2, PW - GW // 2)
            src, dst = opart.at[yy, :, :, at], ry.at[order - 1, :, :, at]
            go(rdma(src, dst, rys.at[part, order - 1], ryr.at[part, order - 1], me.at_y(order)))

        pair(0)
        pair(1)
        if order:
            ship(0)
        ring_tick(me, go, 5 + turn, wall, ws, wr)
        pair(2)
        pair(3)
        opart[yy, :, :, GW:] = pack_lse(lse_buf[...], False).reshape(NZ, ROWS, 128)
        if order:
            ship(1)

    ring_tick(me, go, 9, wall, ws, wr)
    ring_tick(me, go, 10, wall, ws, wr)
    items = [opart[me.y].reshape(nrow, PW)]
    for d in (2, 1, 3):
        for part, at in ((0, pl.ds(0, GW // 2)), (1, pl.ds(GW // 2, PW - GW // 2))):
            blk = ry.at[d - 1, :, :, at]
            rdma(blk, blk, rys.at[part, d - 1], ryr.at[part, d - 1], me.at_y(d)).wait_recv()
        items.append(ry[d - 1].reshape(nrow, PW))
    mg[...] = join_partials(items).reshape(NZ, ROWS, PW)
    for d in (4, 3, 5, 2, 6, 1, 7):
        go(rdma(mg.at[me.zz(d)], rz.at[d - 1], rzs.at[d - 1], rzr.at[d - 1], me.at_z(d)))
    ring_tick(me, go, 11, wall, ws, wr)
    items = [mg[me.z]]
    for d in range(1, NZ):
        blk = rz.at[d - 1]
        rdma(blk, blk, rzs.at[d - 1], rzr.at[d - 1], me.at_z(d)).wait_recv()
        items.append(rz[d - 1])
    att = join_partials(items, final=True)
    ring_tick(me, go, 12, wall, ws, wr)
    ring_tick(me, go, 13, wall, ws, wr)

    plane = [(dy, dv) for dv in (4, 3, 5, 2, 6, 1, 7, 0) for dy in (2, 1, 3, 0)][:-1]
    for j in range(NY):
        tin[0, j] = att[:, j * FEAT : (j + 1) * FEAT]
    aall[me.v, me.y] = tin[0, me.y]
    for dy, dv in plane:
        dev = (me.z * NY + me.yy(dy), lax.rem(me.v + dv, NV))
        go(rdma(tin.at[0, me.yy(dy)], aall.at[me.v, me.y], avs.at[dv, dy], avr.at[dv, dy], dev))
    tok = NY * ROWS
    for dy, dv in reversed(plane):
        blk = aall.at[lax.rem(me.v - dv + NV, NV), me.yy(-dy)]
        rdma(blk, blk, avs.at[dv, dy], avr.at[dv, dy], me.at_y(1)).wait_recv()
    ring_wait(me, wall, ws, wr)
    lhs = jnp.concatenate([aall[g].reshape(tok, FEAT) for g in range(NV)], axis=1)
    proj = jnp.dot(lhs, wall[...].reshape(NV * FEAT, GW), preferred_element_type=F32)
    ppart[...] = proj.astype(BF).reshape(NY, ROWS, GW)
    for d in (2, 1, 3):
        go(rdma(ppart.at[me.yy(d)], rp.at[d - 1], ps_.at[d - 1], pr_.at[d - 1], me.at_y(d)))
    for cp in later[1:3]:
        cp.wait()
    total = res_ref[...].astype(F32) + ppart[me.y].astype(F32)
    for d in (1, 3, 2):
        blk = rp.at[d - 1]
        rdma(blk, blk, ps_.at[d - 1], pr_.at[d - 1], me.at_y(d)).wait_recv()
        total = total + rp[d - 1].astype(F32)
    hidden = total.astype(BF)
    hid_ref[...] = hidden

    wide = hidden.astype(F32)
    sq[me.v] = jnp.broadcast_to(jnp.sum(wide * wide, axis=1, keepdims=True), (ROWS, 128))
    for d in (4, 3, 5, 2, 6, 1, 7):
        go(rdma(sq.at[me.v], sq.at[me.v], sqs.at[d - 1], sqr.at[d - 1], me.at_v(d)))
    for d in range(1, NV):
        blk = sq.at[lax.rem(me.v - d + NV, NV)]
        rdma(blk, blk, sqs.at[d - 1], sqr.at[d - 1], me.at_v(1)).wait_recv()
    mean = jnp.sum(sq[...], axis=0)[:, :1] * (1.0 / D)
    nall[me.y, me.z] = (wide * lax.rsqrt(mean + EPSILON) * gain_ref[...]).astype(BF)
    gather_start(me, go, nall, hz, hzr)
    for cp in later[:1] + later[3:]:
        cp.wait()

    shift = (2, 1, 3, 0)
    for d in (0, 1, 7, 2, 6, 3, 5, 4):
        gather_pass(me, go, nall, me.zz(d), d == 0, hz, hzr, hy, hyr)

    def multiply(o):
        yy = me.yy(-o)
        if o:
            for d in (0, 1, 7, 2, 6, 3, 5, 4):
                gather_wait(me, nall, o, me.zz(d), hy, hyr)
        blocks = [nall[yy, me.xx(d) * 2 + core] for core in (1 - me.c, me.c) for d in shift]
        lhs = jnp.concatenate(blocks, axis=0)
        for n in range(NT):
            at = pl.ds(n * TILE, TILE)
            both = jnp.dot(lhs, hw_ref[:, at], preferred_element_type=F32)
            osend[o, :, :, at] = both[:tok].astype(BF).reshape(NX, ROWS, TILE)
            own[o, :, :, at] = both[tok:].reshape(NX, ROWS, TILE)
        go(rdma(osend.at[o], orecv.at[o], cs.at[o], cr.at[o], me.at_x(0, 1 - me.c)))

    def pass_on(o):
        rdma(orecv.at[o], orecv.at[o], cs.at[o], cr.at[o], me.at_x(0, 1 - me.c)).wait_recv()
        for i, d in enumerate(shift[:3]):
            sx[o, i] = (own[o, i] + orecv[o, i].astype(F32)).astype(BF)
            go(rdma(sx.at[o, i], x2.at[o, i], xs.at[o, i], xr.at[o, i], me.at_x(d, me.c)))
        at = pl.ds(pl.multiple_of(me.yy(-o) * ROWS, ROWS), ROWS)
        final[at] = own[o, 3] + orecv[o, 3].astype(F32)

    turns = (0, 1, 3, 2)
    multiply(turns[0])
    for before, o in zip(turns, turns[1:]):
        pass_on(before)
        multiply(o)
    pass_on(turns[3])

    tgt = jnp.concatenate([tgt_ref[...], jnp.zeros((1, 128 - tok), jnp.int32)], axis=1)
    tgt = jnp.broadcast_to(tgt.astype(F32), (128, 128))
    tgt = jnp.transpose(tgt)[:tok, :1].astype(jnp.int32) - me.s * VOC
    peak = None
    for o in turns:
        at = pl.ds(pl.multiple_of(me.yy(-o) * ROWS, ROWS), ROWS)
        lg = final[at]
        for i in range(3):
            rdma(x2.at[o, i], x2.at[o, i], xs.at[o, i], xr.at[o, i], me.at_x(1, me.c)).wait_recv()
            lg = lg + x2[o, i].astype(F32)
        final[at] = lg
    for n in range(NT):
        at = pl.ds(n * TILE, TILE)
        lg = final[:, at]
        top = jnp.max(lg, axis=1, keepdims=True)
        peak = top if peak is None else jnp.maximum(peak, top)
    total = picked = None
    for n in range(NT):
        lg = final[:, pl.ds(n * TILE, TILE)]
        a = jnp.sum(jnp.exp(lg - peak), axis=1, keepdims=True)
        b = jnp.sum(jnp.where(lanes((tok, TILE)) + n * TILE == tgt, lg, 0.0), axis=1, keepdims=True)
        total = a if total is None else total + a
        picked = b if picked is None else picked + b
    lane = lanes((tok, 128))
    st = jnp.where(lane == 0, peak, jnp.where(lane == 1, total, picked))
    st = jnp.concatenate([st, jnp.zeros((128 - tok, 128), F32)], axis=0)
    sty[0] = jnp.transpose(st)[:8]

    def joined(buf, count):
        top = functools.reduce(jnp.maximum, [buf[i, 0:1] for i in range(count)])
        tot = functools.reduce(jnp.add, [buf[i, 1:2] * jnp.exp(buf[i, 0:1] - top) for i in range(count)])
        pick = functools.reduce(jnp.add, [buf[i, 2:3] for i in range(count)])
        return top, tot, pick

    for d in (2, 1, 3):
        go(rdma(sty.at[0], sty.at[d], yss.at[d - 1], yrs.at[d - 1], me.at_y(d)))
    for d in range(1, NY):
        rdma(sty.at[d], sty.at[d], yss.at[d - 1], yrs.at[d - 1], me.at_y(d)).wait_recv()
    top, tot, pick = joined(sty, NY)
    stz[0] = jnp.concatenate([top, tot, pick, jnp.zeros((5, 128), F32)], axis=0)
    for d in (4, 3, 5, 2, 6, 1, 7):
        go(rdma(stz.at[0], stz.at[d], zss.at[d - 1], zrs.at[d - 1], me.at_z(d)))
    for d in range(1, NZ):
        rdma(stz.at[d], stz.at[d], zss.at[d - 1], zrs.at[d - 1], me.at_z(d)).wait_recv()
    top, tot, pick = joined(stz, NZ)
    out_ref[...] = (pick - (top + jnp.log(tot)))[:, :tok]
    for cp in sends:
        cp.wait_send()


def vm():
    return pl.BlockSpec(memory_space=pltpu.VMEM)


def params(cid):
    return pltpu.CompilerParams(
        collective_id=cid, has_side_effects=True, vmem_limit_bytes=56 * 1024 * 1024
    )


def dma(*shape):
    return pltpu.SemaphoreType.DMA(shape)


def shards(q, sk, sv, ck, cv, start, w, res, gain, hw, tgt):
    any_ = pl.BlockSpec(memory_space=pl.ANY)
    tok = NY * ROWS
    hidden, logprobs = pl.pallas_call(
        kernel,
        out_shape=(
            jax.ShapeDtypeStruct((ROWS, GW), BF),
            jax.ShapeDtypeStruct((1, tok), F32),
        ),
        in_specs=[any_] * 5 + [pl.BlockSpec(memory_space=pltpu.SMEM)] + [any_] * 5,
        out_specs=(vm(), vm()),
        scratch_shapes=[
            pltpu.VMEM((NY, NZ, ROWS, GW), BF),
            pltpu.VMEM((KEYS_PAD, HS), BF),
            pltpu.VMEM((KEYS_PAD, HS), BF),
            pltpu.VMEM((KEYS_PAD, 2 * HS), BF),
            pltpu.VMEM((1, KEYS_PAD), F32),
            pltpu.VMEM((NZ * ROWS, 128), F32),
            pltpu.VMEM((NY, NZ, ROWS, PW), BF),
            pltpu.VMEM((NY - 1, NZ, ROWS, PW), BF),
            pltpu.VMEM((NZ, ROWS, PW), BF),
            pltpu.VMEM((NZ - 1, ROWS, PW), BF),
            pltpu.VMEM((NZ, FEAT, GW), BF),
            pltpu.VMEM((GW, VOC), BF),
            pltpu.VMEM((ROWS, GW), BF),
            pltpu.VMEM((1, GW), F32),
            pltpu.VMEM((1, tok), jnp.int32),
            pltpu.VMEM((1, NY, ROWS, FEAT), BF),
            pltpu.VMEM((NV, NY, ROWS, FEAT), BF),
            pltpu.VMEM((NY, ROWS, GW), BF),
            pltpu.VMEM((NY - 1, ROWS, GW), BF),
            pltpu.VMEM((NV, ROWS, 128), F32),
            pltpu.VMEM((NY, NZ, ROWS, GW), BF),
            pltpu.VMEM((NY, NX, ROWS, VOC), BF),
            pltpu.VMEM((NY, NX, ROWS, VOC), BF),
            pltpu.VMEM((NY, NX, ROWS, VOC), F32),
            pltpu.VMEM((tok, VOC), F32),
            pltpu.VMEM((NY, NX - 1, ROWS, VOC), BF),
            pltpu.VMEM((NY, NX - 1, ROWS, VOC), BF),
            pltpu.VMEM((NY, 8, 128), F32),
            pltpu.VMEM((NZ, 8, 128), F32),
            dma(8), dma(2, NV - 1), dma(NV), dma(NV),
            dma(NZ - 1), dma(NZ), dma(NY - 1, NZ), dma(NY - 1, NZ),
            dma(2, len(TICKS)), dma(2, NZ // 2 * PIECES),
            dma(2, NY - 1), dma(2, NY - 1), dma(NZ - 1), dma(NZ - 1),
            dma(NV, NY), dma(NV, NY),
            dma(NY - 1), dma(NY - 1), dma(NV - 1), dma(NV - 1),
            dma(NZ - 1), dma(NZ), dma(NY - 1, NZ), dma(NY - 1, NZ),
            dma(NY), dma(NY), dma(NY, NX - 1), dma(NY, NX - 1),
            dma(NY - 1), dma(NY - 1), dma(NZ - 1), dma(NZ - 1),
        ],
        compiler_params=params(0),
        name="layer",
    )(q, sk, sv, ck, cv, start, w, res, gain.reshape(1, GW), hw, tgt.reshape(1, tok))
    return hidden, logprobs.reshape(tok)


def solution(mesh):
    placed = (
        P("seq", None),
        P("seq", None),
        P("seq", None),
        P(("seq", "vocab"), None),
        P(("seq", "vocab"), None),
        P(),
        P("seq", "vocab"),
        P("seq", "vocab"),
        P("vocab"),
        P("vocab", "seq"),
        P("vocab"),
    )
    return jax.shard_map(
        shards,
        mesh=mesh,
        in_specs=placed,
        out_specs=(P("seq", "vocab"), P("vocab")),
        check_vma=False,
    )
```

```python
import functools
import math

import jax
import jax.numpy as jnp
from jax import lax
from jax.experimental import pallas as pl
from jax.experimental.pallas import tpu as pltpu
from jax.sharding import PartitionSpec as P

D = 8192
HEADS = 8
HS = 128
NY, NZ, NX = 4, 8, 4
NV = 2 * NX
ROWS = 16
CACHE = 256
KEYS = NV * CACHE
KEYS_PAD = KEYS + 128
GW = HEADS * HS
PW = GW + 128
VOC = 2048
TILE = 512
NT = VOC // TILE
FEAT = 256
BIG_NEG = -1e30
EPSILON = 1e-05
MESH = pl.DeviceIdType.MESH
BF = jnp.bfloat16
F32 = jnp.float32


class Place:
    def __init__(self):
        s, v = lax.axis_index("seq"), lax.axis_index("vocab")
        self.s, self.v = s, v
        self.z, self.y = lax.div(s, NY), lax.rem(s, NY)
        self.x, self.c = lax.div(v, 2), lax.rem(v, 2)

    def yy(self, d):
        return lax.rem(self.y + d + NY, NY)

    def zz(self, d):
        return lax.rem(self.z + d + NZ, NZ)

    def xx(self, d):
        return lax.rem(self.x + d + NX, NX)

    def at_z(self, d):
        return (self.zz(d) * NY + self.y, self.v)

    def at_y(self, d):
        return (self.z * NY + self.yy(d), self.v)

    def at_x(self, d, core):
        return (self.s, self.xx(d) * 2 + core)

    def at_v(self, d):
        return (self.s, lax.rem(self.v + d, NV))


def rdma(src, dst, send, recv, dev):
    return pltpu.make_async_remote_copy(
        src_ref=src, dst_ref=dst, send_sem=send, recv_sem=recv, device_id=dev, device_id_type=MESH
    )


def greet(partners):
    bar = pltpu.get_barrier_semaphore()
    for dev in partners:
        pl.semaphore_signal(bar, inc=1, device_id=dev, device_id_type=MESH)


def gather_start(me, go, buf, zs, zr):
    own = buf.at[me.y, me.z]
    for d in (1, 7, 2, 6, 3, 5, 4):
        go(rdma(own, own, zs.at[d - 1], zr.at[me.z], me.at_z(d)))


def gather_pass(me, go, buf, src, own, zs, zr, ys, yr):
    blk = buf.at[me.y, src]
    if not own:
        rdma(blk, blk, zs.at[0], zr.at[src], me.at_z(1)).wait_recv()
    for e in (2, 1, 3):
        go(rdma(blk, blk, ys.at[e - 1, src], yr.at[e - 1, src], me.at_y(e)))


def gather_wait(me, buf, e, src, ys, yr):
    blk = buf.at[me.yy(-e), src]
    rdma(blk, blk, ys.at[e - 1, src], yr.at[e - 1, src], me.at_y(e)).wait_recv()


PIECES = 4
TICKS = [(step, p) for step in range(NZ // 2 - 1) for p in range(PIECES)]
TICKS += [(NZ // 2 - 1, p) for p in range(PIECES // 2)]


def ring_piece(me, buf, k, way, step, p):
    rows = buf.shape[1] // PIECES
    p = p + k * (PIECES // 2) if step == NZ // 2 - 1 else p
    return buf.at[me.zz(-way * step), pl.ds(p * rows, rows)], p


def ring_tick(me, go, tick, buf, ss, rs):
    step, p0 = TICKS[tick]
    for k, way in ((0, 1), (1, -1)):
        blk, p = ring_piece(me, buf, k, way, step, p0)
        if step:
            rdma(blk, blk, ss.at[k, 0], rs.at[k, (step - 1) * PIECES + p], me.at_z(way)).wait_recv()
        go(rdma(blk, blk, ss.at[k, tick], rs.at[k, step * PIECES + p], me.at_z(way)))


def ring_wait(me, buf, ss, rs):
    last = NZ // 2 - 1
    rows = buf.shape[1] // PIECES
    for k, way in ((0, 1), (1, -1)):
        for p in range(PIECES):
            if p // (PIECES // 2) == k:
                blk = buf.at[me.zz(-way * (last + 1)), pl.ds(p * rows, rows)]
                rdma(blk, blk, ss.at[k, 0], rs.at[k, last * PIECES + p], me.at_z(way)).wait_recv()
            else:
                blk = buf.at[me.zz(-way * last), pl.ds(p * rows, rows)]
                rdma(blk, blk, ss.at[k, 0], rs.at[k, (last - 1) * PIECES + p], me.at_z(way)).wait_recv()


def lanes(shape):
    return lax.broadcasted_iota(jnp.int32, shape, len(shape) - 1)


def pack_lse(lse, low8):
    second = pltpu.roll(lse, 8, 1) if low8 else lse
    third = pltpu.roll(lse, 16, 1) if low8 else lse

    def split(a):
        hi = a.astype(BF).astype(F32)
        mid = (a - hi).astype(BF).astype(F32)
        return hi, mid, a - hi - mid

    lane = lanes(lse.shape)
    out = jnp.where(lane < 8, split(lse)[0], jnp.where(lane < 16, split(second)[1], split(third)[2]))
    return jnp.where(lane < 24, out, 0.0).astype(BF)


def unpack_lse(packed):
    a = packed.astype(F32)
    return a + (pltpu.roll(a, 120, 1) + pltpu.roll(a, 112, 1))


def join_partials(items, final=False):
    lses = [unpack_lse(it[:, GW:]) for it in items]
    peak = functools.reduce(jnp.maximum, lses)
    weights = [jnp.exp2(l - peak) for l in lses]
    total = functools.reduce(jnp.add, weights)
    weights = [w / total for w in weights]
    cols = []
    for h in range(HEADS):
        acc = None
        for w, it in zip(weights, items):
            term = w[:, h : h + 1] * it[:, h * HS : (h + 1) * HS].astype(F32)
            acc = term if acc is None else acc + term
        cols.append(acc.astype(BF))
    if not final:
        cols.append(pack_lse(peak + jnp.log2(total), True))
    return jnp.concatenate(cols, axis=1)


def kernel(
    q_ref, sk_ref, sv_ref, ck_ref, cv_ref, start_ref, w_ref, res_hbm, gain_hbm, hw_hbm, tgt_hbm,
    hid_ref, out_ref,
    qall, kbuf, vbuf, vext, bias, lse_buf, opart, ry, mg, rz, wall, hw_ref, res_ref, gain_ref, tgt_ref, tin, aall, ppart, rp, sq, nall, scy, scz, scale_of,
    osend, orecv, own, final, sx, x2, sty, stz,
    loc, kvs, kr, vr, gz, gzr, gy, gyr, ws, wr, rys, ryr, rzs, rzr, avs, avr, ps_, pr_, sqs, sqr, scs, scr, sczs, sczr,
    hz, hzr, hy, hyr, cs, cr, xs, xr, yss, yrs, zss, zrs,
):
    me = Place()
    sends = []

    def go(cp):
        cp.start()
        sends.append(cp)

    def cols(vv):
        return pl.ds(pl.multiple_of(vv * HS, HS), HS)

    def rows(vv):
        return pl.ds(pl.multiple_of(vv * CACHE, CACHE), CACHE)

    greet(
        [me.at_z(d) for d in range(1, NZ)]
        + [
            (me.z * NY + me.yy(dy), lax.rem(me.v + dv, NV))
            for dy in range(NY)
            for dv in range(NV)
            if dy or dv
        ]
    )

    def fetch(src, dst, sem):
        cp = pltpu.make_async_copy(src, dst, sem)
        cp.start()
        return cp

    head_cols = pl.ds(pl.multiple_of(me.v * GW, GW), GW)
    own_q = fetch(q_ref.at[:, head_cols], qall.at[me.y, me.z], loc.at[0])
    own_w = fetch(w_ref, wall.at[me.z], loc.at[1])
    own_k = fetch(ck_ref.at[:, cols(me.v)], kbuf.at[rows(me.v)], kr.at[me.v])
    own_v = fetch(cv_ref.at[:, cols(me.v)], vbuf.at[rows(me.v)], vr.at[me.v])
    span_k = fetch(sk_ref.at[:, cols(me.v)], kbuf.at[pl.ds(KEYS, ROWS)], loc.at[3])
    span_v = fetch(sv_ref.at[:, cols(me.v)], vbuf.at[pl.ds(KEYS, ROWS)], loc.at[4])
    later = [fetch(hw_hbm, hw_ref, loc.at[2]), fetch(res_hbm, res_ref, loc.at[5])]
    later += [fetch(gain_hbm, gain_ref, loc.at[6]), fetch(tgt_hbm, tgt_ref, loc.at[7])]
    kbuf[KEYS + ROWS :, :] = jnp.zeros((128 - ROWS, HS), BF)
    vbuf[KEYS + ROWS :, :] = jnp.zeros((128 - ROWS, HS), BF)
    flat = lanes((1, KEYS_PAD))
    bias[...] = jnp.where(flat < start_ref[0] - me.s * KEYS, 0.0, BIG_NEG)
    own_q.wait()
    own_w.wait()
    pl.semaphore_wait(pltpu.get_barrier_semaphore(), NZ - 1 + NY * NV - 1)

    gather_start(me, go, qall, gz, gzr)
    for i, d in enumerate((4, 3, 5, 2, 6, 1, 7)):
        vv = lax.rem(me.v + d, NV)
        go(rdma(ck_ref.at[:, cols(vv)], kbuf.at[rows(me.v)], kvs.at[0, i], kr.at[me.v], me.at_v(d)))
        go(rdma(cv_ref.at[:, cols(vv)], vbuf.at[rows(me.v)], kvs.at[1, i], vr.at[me.v], me.at_v(d)))
    ring_tick(me, go, 0, wall, ws, wr)
    ring_tick(me, go, 1, wall, ws, wr)
    for d in (0, 1, 7, 2, 6, 3, 5, 4):
        gather_pass(me, go, qall, me.zz(d), d == 0, gz, gzr, gy, gyr)
    ring_tick(me, go, 2, wall, ws, wr)
    ring_tick(me, go, 3, wall, ws, wr)
    span_k.wait()
    span_v.wait()
    own_k.wait()
    own_v.wait()
    for d in range(1, NV):
        src = lax.rem(me.v + d, NV)
        blk = kbuf.at[rows(src)]
        rdma(blk, blk, kvs.at[0, 0], kr.at[src], me.at_v(1)).wait_recv()
        blk = vbuf.at[rows(src)]
        rdma(blk, blk, kvs.at[1, 0], vr.at[src], me.at_v(1)).wait_recv()
    vext[:, :HS] = vbuf[...]
    vext[:, HS:] = jnp.ones((KEYS_PAD, HS), BF)
    ring_tick(me, go, 4, wall, ws, wr)

    scale = math.log2(math.e) / math.sqrt(HS)
    nrow = NZ * ROWS
    for turn, order in enumerate((2, 1, 3, 0)):
        yy = me.yy(order)
        if order:
            for d in (0, 1, 7, 2, 6, 3, 5, 4):
                gather_wait(me, qall, NY - order, me.zz(d), gy, gyr)

        def pair(hp):
            both = []
            for i in range(2):
                at = pl.ds((hp * 2 + i) * HS, HS)
                both.append(qall[yy, :, :, at].reshape(nrow, HS))
            q2 = jnp.concatenate(both, axis=0)
            sc = lax.dot_general(q2, kbuf[...], (((1,), (1,)), ((), ())), preferred_element_type=F32)
            main = sc[:, :KEYS] * scale + bias[:, :KEYS]
            row = lax.broadcasted_iota(jnp.int32, (2 * nrow, 128), 0)
            row = lax.rem(row, nrow)
            token = lax.div(row, ROWS) * (NY * ROWS) + yy * ROWS + lax.rem(row, ROWS)
            key = lanes((2 * nrow, 128))
            ok = (key < ROWS) & (key + me.s * ROWS <= token)
            span = jnp.where(ok, sc[:, KEYS:] * scale, BIG_NEG)
            peak = jnp.maximum(
                jnp.max(main, axis=1, keepdims=True), jnp.max(span, axis=1, keepdims=True)
            )
            pm = jnp.exp2(main - peak).astype(BF)
            ps = jnp.exp2(span - peak).astype(BF)
            ps = jnp.where(ok, ps, jnp.zeros_like(ps))
            o = jnp.dot(pm, vext[:KEYS, :], preferred_element_type=F32)
            o = o + jnp.dot(ps, vext[KEYS:, :], preferred_element_type=F32)
            total = o[:, HS:]
            total = jnp.where(total > 0.0, total, 1.0)
            on = (o[:, :HS] / total).astype(BF)
            lse = peak + jnp.log2(total)
            lane = lanes((nrow, 128))
            for i in range(2):
                h = hp * 2 + i
                at = pl.ds(h * HS, HS)
                opart[yy, :, :, at] = on[i * nrow : (i + 1) * nrow].reshape(NZ, ROWS, HS)
                mine = lse[i * nrow : (i + 1) * nrow]
                lse_buf[...] = jnp.where(lax.rem(lane, 8) == h, mine, lse_buf[...])

        def ship(part):
            at = pl.ds(0, GW // 2) if part == 0 else pl.ds(GW // 2, PW - GW // 2)
            src, dst = opart.at[yy, :, :, at], ry.at[order - 1, :, :, at]
            go(rdma(src, dst, rys.at[part, order - 1], ryr.at[part, order - 1], me.at_y(order)))

        pair(0)
        pair(1)
        if order:
            ship(0)
        ring_tick(me, go, 5 + turn, wall, ws, wr)
        pair(2)
        pair(3)
        opart[yy, :, :, GW:] = pack_lse(lse_buf[...], False).reshape(NZ, ROWS, 128)
        if order:
            ship(1)

    ring_tick(me, go, 9, wall, ws, wr)
    ring_tick(me, go, 10, wall, ws, wr)
    items = [opart[me.y].reshape(nrow, PW)]
    for d in (2, 1, 3):
        for part, at in ((0, pl.ds(0, GW // 2)), (1, pl.ds(GW // 2, PW - GW // 2))):
            blk = ry.at[d - 1, :, :, at]
            rdma(blk, blk, rys.at[part, d - 1], ryr.at[part, d - 1], me.at_y(d)).wait_recv()
        items.append(ry[d - 1].reshape(nrow, PW))
    mg[...] = join_partials(items).reshape(NZ, ROWS, PW)
    for d in (4, 3, 5, 2, 6, 1, 7):
        go(rdma(mg.at[me.zz(d)], rz.at[d - 1], rzs.at[d - 1], rzr.at[d - 1], me.at_z(d)))
    ring_tick(me, go, 11, wall, ws, wr)
    items = [mg[me.z]]
    for d in range(1, NZ):
        blk = rz.at[d - 1]
        rdma(blk, blk, rzs.at[d - 1], rzr.at[d - 1], me.at_z(d)).wait_recv()
        items.append(rz[d - 1])
    att = join_partials(items, final=True)
    ring_tick(me, go, 12, wall, ws, wr)
    ring_tick(me, go, 13, wall, ws, wr)

    plane = [(dy, dv) for dv in (4, 3, 5, 2, 6, 1, 7, 0) for dy in (2, 1, 3, 0)][:-1]
    for j in range(NY):
        tin[0, j] = att[:, j * FEAT : (j + 1) * FEAT]
    aall[me.v, me.y] = tin[0, me.y]
    for dy, dv in plane:
        dev = (me.z * NY + me.yy(dy), lax.rem(me.v + dv, NV))
        go(rdma(tin.at[0, me.yy(dy)], aall.at[me.v, me.y], avs.at[dv, dy], avr.at[dv, dy], dev))
    tok = NY * ROWS
    for dy, dv in reversed(plane):
        blk = aall.at[lax.rem(me.v - dv + NV, NV), me.yy(-dy)]
        rdma(blk, blk, avs.at[dv, dy], avr.at[dv, dy], me.at_y(1)).wait_recv()
    ring_wait(me, wall, ws, wr)
    lhs = jnp.concatenate([aall[g].reshape(tok, FEAT) for g in range(NV)], axis=1)
    proj = jnp.dot(lhs, wall[...].reshape(NV * FEAT, GW), preferred_element_type=F32)
    ppart[...] = proj.astype(BF).reshape(NY, ROWS, GW)
    for d in (2, 1, 3):
        go(rdma(ppart.at[me.yy(d)], rp.at[d - 1], ps_.at[d - 1], pr_.at[d - 1], me.at_y(d)))
    for cp in later[1:3]:
        cp.wait()
    total = res_ref[...].astype(F32) + ppart[me.y].astype(F32)
    for d in (1, 3, 2):
        blk = rp.at[d - 1]
        rdma(blk, blk, ps_.at[d - 1], pr_.at[d - 1], me.at_y(d)).wait_recv()
        total = total + rp[d - 1].astype(F32)
    hidden = total.astype(BF)
    hid_ref[...] = hidden

    nall[me.y, me.z] = hidden
    gather_start(me, go, nall, hz, hzr)
    wide = hidden.astype(F32)
    sq[me.v] = jnp.broadcast_to(jnp.sum(wide * wide, axis=1, keepdims=True), (ROWS, 128))
    for d in (4, 3, 5, 2, 6, 1, 7):
        go(rdma(sq.at[me.v], sq.at[me.v], sqs.at[d - 1], sqr.at[d - 1], me.at_v(d)))
    gather_pass(me, go, nall, me.z, True, hz, hzr, hy, hyr)
    for d in range(1, NV):
        blk = sq.at[lax.rem(me.v - d + NV, NV)]
        rdma(blk, blk, sqs.at[d - 1], sqr.at[d - 1], me.at_v(1)).wait_recv()
    mean = jnp.sum(sq[...], axis=0) * (1.0 / D)
    spread = jnp.transpose(jnp.concatenate([lax.rsqrt(mean + EPSILON)] * (128 // ROWS), axis=0))[:8]
    scy[0] = jnp.where(lax.div(lanes((8, 128)), ROWS) == me.y, spread, 0.0)
    for d in (2, 1, 3):
        go(rdma(scy.at[0], scy.at[d], scs.at[d - 1], scr.at[d - 1], me.at_y(d)))
    for d in (1, 7):
        gather_pass(me, go, nall, me.zz(d), False, hz, hzr, hy, hyr)
    for d in (2, 1, 3):
        rdma(scy.at[d], scy.at[d], scs.at[d - 1], scr.at[d - 1], me.at_y(d)).wait_recv()
    scz[me.z] = scy[0] + scy[1] + scy[2] + scy[3]
    for d in (4, 3, 5, 2, 6, 1, 7):
        go(rdma(scz.at[me.z], scz.at[me.z], sczs.at[d - 1], sczr.at[me.z], me.at_z(d)))
    for d in (2, 6, 3, 5, 4):
        gather_pass(me, go, nall, me.zz(d), False, hz, hzr, hy, hyr)
    for d in range(1, NZ):
        blk = scz.at[me.zz(d)]
        rdma(blk, blk, sczs.at[0], sczr.at[me.zz(d)], me.at_z(1)).wait_recv()
    turned = [scz[i, 0:1] for i in range(NZ)] + [jnp.zeros((128 - NZ, 128), F32)]
    scale_of[...] = jnp.transpose(jnp.concatenate(turned, axis=0))
    for cp in later[:1] + later[3:]:
        cp.wait()

    shift = (2, 1, 3, 0)

    def multiply(o):
        yy = me.yy(-o)
        if o:
            for d in (0, 1, 7, 2, 6, 3, 5, 4):
                gather_wait(me, nall, o, me.zz(d), hy, hyr)
        scales = scale_of[pl.ds(pl.multiple_of(yy * ROWS, ROWS), ROWS)]
        blocks = []
        for core in (1 - me.c, me.c):
            for d in shift:
                zz = me.xx(d) * 2 + core
                rs = jnp.where(lanes((ROWS, 128)) == zz, scales, 0.0)
                rs = jnp.sum(rs, axis=1, keepdims=True)
                blocks.append((nall[yy, zz].astype(F32) * rs * gain_ref[...]).astype(BF))
        lhs = jnp.concatenate(blocks, axis=0)
        for n in range(NT):
            at = pl.ds(n * TILE, TILE)
            both = jnp.dot(lhs, hw_ref[:, at], preferred_element_type=F32)
            osend[o, :, :, at] = both[:tok].astype(BF).reshape(NX, ROWS, TILE)
            own[o, :, :, at] = both[tok:].reshape(NX, ROWS, TILE)
        go(rdma(osend.at[o], orecv.at[o], cs.at[o], cr.at[o], me.at_x(0, 1 - me.c)))

    def pass_on(o):
        rdma(orecv.at[o], orecv.at[o], cs.at[o], cr.at[o], me.at_x(0, 1 - me.c)).wait_recv()
        for i, d in enumerate(shift[:3]):
            sx[o, i] = (own[o, i] + orecv[o, i].astype(F32)).astype(BF)
            go(rdma(sx.at[o, i], x2.at[o, i], xs.at[o, i], xr.at[o, i], me.at_x(d, me.c)))
        at = pl.ds(pl.multiple_of(me.yy(-o) * ROWS, ROWS), ROWS)
        final[at] = own[o, 3] + orecv[o, 3].astype(F32)

    turns = (0, 1, 3, 2)
    multiply(turns[0])
    for before, o in zip(turns, turns[1:]):
        pass_on(before)
        multiply(o)
    pass_on(turns[3])

    tgt = jnp.concatenate([tgt_ref[...], jnp.zeros((1, 128 - tok), jnp.int32)], axis=1)
    tgt = jnp.broadcast_to(tgt.astype(F32), (128, 128))
    tgt = jnp.transpose(tgt)[:tok, :1].astype(jnp.int32) - me.s * VOC
    peak = None
    for o in turns:
        at = pl.ds(pl.multiple_of(me.yy(-o) * ROWS, ROWS), ROWS)
        lg = final[at]
        for i in range(3):
            rdma(x2.at[o, i], x2.at[o, i], xs.at[o, i], xr.at[o, i], me.at_x(1, me.c)).wait_recv()
            lg = lg + x2[o, i].astype(F32)
        final[at] = lg
    for n in range(NT):
        at = pl.ds(n * TILE, TILE)
        lg = final[:, at]
        top = jnp.max(lg, axis=1, keepdims=True)
        peak = top if peak is None else jnp.maximum(peak, top)
    total = picked = None
    for n in range(NT):
        lg = final[:, pl.ds(n * TILE, TILE)]
        a = jnp.sum(jnp.exp(lg - peak), axis=1, keepdims=True)
        b = jnp.sum(jnp.where(lanes((tok, TILE)) + n * TILE == tgt, lg, 0.0), axis=1, keepdims=True)
        total = a if total is None else total + a
        picked = b if picked is None else picked + b
    lane = lanes((tok, 128))
    st = jnp.where(lane == 0, peak, jnp.where(lane == 1, total, picked))
    st = jnp.concatenate([st, jnp.zeros((128 - tok, 128), F32)], axis=0)
    sty[0] = jnp.transpose(st)[:8]

    def joined(buf, count):
        top = functools.reduce(jnp.maximum, [buf[i, 0:1] for i in range(count)])
        tot = functools.reduce(jnp.add, [buf[i, 1:2] * jnp.exp(buf[i, 0:1] - top) for i in range(count)])
        pick = functools.reduce(jnp.add, [buf[i, 2:3] for i in range(count)])
        return top, tot, pick

    for d in (2, 1, 3):
        go(rdma(sty.at[0], sty.at[d], yss.at[d - 1], yrs.at[d - 1], me.at_y(d)))
    for d in range(1, NY):
        rdma(sty.at[d], sty.at[d], yss.at[d - 1], yrs.at[d - 1], me.at_y(d)).wait_recv()
    top, tot, pick = joined(sty, NY)
    stz[0] = jnp.concatenate([top, tot, pick, jnp.zeros((5, 128), F32)], axis=0)
    for d in (4, 3, 5, 2, 6, 1, 7):
        go(rdma(stz.at[0], stz.at[d], zss.at[d - 1], zrs.at[d - 1], me.at_z(d)))
    for d in range(1, NZ):
        rdma(stz.at[d], stz.at[d], zss.at[d - 1], zrs.at[d - 1], me.at_z(d)).wait_recv()
    top, tot, pick = joined(stz, NZ)
    out_ref[...] = (pick - (top + jnp.log(tot)))[:, :tok]
    for cp in sends:
        cp.wait_send()


def hand_over(hid_ref, logprob_ref, hid_out, logprob_out):
    hid_out[...] = hid_ref[...]
    logprob_out[...] = logprob_ref[0, :]


def vm():
    return pl.BlockSpec(memory_space=pltpu.VMEM)


def params(cid):
    return pltpu.CompilerParams(
        collective_id=cid, has_side_effects=True, vmem_limit_bytes=56 * 1024 * 1024
    )


def dma(*shape):
    return pltpu.SemaphoreType.DMA(shape)


def shards(q, sk, sv, ck, cv, start, w, res, gain, hw, tgt):
    any_ = pl.BlockSpec(memory_space=pl.ANY)
    tok = NY * ROWS
    hidden, logprobs = pl.pallas_call(
        kernel,
        out_shape=(
            jax.ShapeDtypeStruct((ROWS, GW), BF),
            jax.ShapeDtypeStruct((1, tok), F32),
        ),
        in_specs=[any_] * 5 + [pl.BlockSpec(memory_space=pltpu.SMEM)] + [any_] * 5,
        out_specs=(vm(), vm()),
        scratch_shapes=[
            pltpu.VMEM((NY, NZ, ROWS, GW), BF),
            pltpu.VMEM((KEYS_PAD, HS), BF),
            pltpu.VMEM((KEYS_PAD, HS), BF),
            pltpu.VMEM((KEYS_PAD, 2 * HS), BF),
            pltpu.VMEM((1, KEYS_PAD), F32),
            pltpu.VMEM((NZ * ROWS, 128), F32),
            pltpu.VMEM((NY, NZ, ROWS, PW), BF),
            pltpu.VMEM((NY - 1, NZ, ROWS, PW), BF),
            pltpu.VMEM((NZ, ROWS, PW), BF),
            pltpu.VMEM((NZ - 1, ROWS, PW), BF),
            pltpu.VMEM((NZ, FEAT, GW), BF),
            pltpu.VMEM((GW, VOC), BF),
            pltpu.VMEM((ROWS, GW), BF),
            pltpu.VMEM((1, GW), F32),
            pltpu.VMEM((1, tok), jnp.int32),
            pltpu.VMEM((1, NY, ROWS, FEAT), BF),
            pltpu.VMEM((NV, NY, ROWS, FEAT), BF),
            pltpu.VMEM((NY, ROWS, GW), BF),
            pltpu.VMEM((NY - 1, ROWS, GW), BF),
            pltpu.VMEM((NV, ROWS, 128), F32),
            pltpu.VMEM((NY, NZ, ROWS, GW), BF),
            pltpu.VMEM((NY, 8, 128), F32),
            pltpu.VMEM((NZ, 8, 128), F32),
            pltpu.VMEM((128, 128), F32),
            pltpu.VMEM((NY, NX, ROWS, VOC), BF),
            pltpu.VMEM((NY, NX, ROWS, VOC), BF),
            pltpu.VMEM((NY, NX, ROWS, VOC), F32),
            pltpu.VMEM((tok, VOC), F32),
            pltpu.VMEM((NY, NX - 1, ROWS, VOC), BF),
            pltpu.VMEM((NY, NX - 1, ROWS, VOC), BF),
            pltpu.VMEM((NY, 8, 128), F32),
            pltpu.VMEM((NZ, 8, 128), F32),
            dma(8), dma(2, NV - 1), dma(NV), dma(NV),
            dma(NZ - 1), dma(NZ), dma(NY - 1, NZ), dma(NY - 1, NZ),
            dma(2, len(TICKS)), dma(2, NZ // 2 * PIECES),
            dma(2, NY - 1), dma(2, NY - 1), dma(NZ - 1), dma(NZ - 1),
            dma(NV, NY), dma(NV, NY),
            dma(NY - 1), dma(NY - 1), dma(NV - 1), dma(NV - 1),
            dma(NY - 1), dma(NY - 1), dma(NZ - 1), dma(NZ),
            dma(NZ - 1), dma(NZ), dma(NY - 1, NZ), dma(NY - 1, NZ),
            dma(NY), dma(NY), dma(NY, NX - 1), dma(NY, NX - 1),
            dma(NY - 1), dma(NY - 1), dma(NZ - 1), dma(NZ - 1),
        ],
        compiler_params=params(0),
        name="layer",
    )(q, sk, sv, ck, cv, start, w, res, gain.reshape(1, GW), hw, tgt.reshape(1, tok))
    return pl.pallas_call(
        hand_over,
        out_shape=(jax.ShapeDtypeStruct((ROWS, GW), BF), jax.ShapeDtypeStruct((tok,), F32)),
        in_specs=[vm(), vm()],
        out_specs=(vm(), vm()),
        name="results",
    )(hidden, logprobs)


def solution(mesh):
    placed = (
        P("seq", None),
        P("seq", None),
        P("seq", None),
        P(("seq", "vocab"), None),
        P(("seq", "vocab"), None),
        P(),
        P("seq", "vocab"),
        P("seq", "vocab"),
        P("vocab"),
        P("vocab", "seq"),
        P("vocab"),
    )
    return jax.shard_map(
        shards,
        mesh=mesh,
        in_specs=placed,
        out_specs=(P("seq", "vocab"), P("vocab")),
        check_vma=False,
    )
```

```python
import functools
import math

import jax
import jax.numpy as jnp
from jax import lax
from jax.experimental import pallas as pl
from jax.experimental.pallas import tpu as pltpu
from jax.sharding import PartitionSpec as P

D = 8192
HEADS = 8
HS = 128
NY, NZ, NX = 4, 8, 4
NV = 2 * NX
ROWS = 16
CACHE = 256
KEYS = NV * CACHE
KEYS_PAD = KEYS + 128
GW = HEADS * HS
PW = GW + 128
VOC = 2048
TILE = 512
NT = VOC // TILE
FEAT = 256
BIG_NEG = -1e30
EPSILON = 1e-05
MESH = pl.DeviceIdType.MESH
BF = jnp.bfloat16
F32 = jnp.float32


class Place:
    def __init__(self):
        s, v = lax.axis_index("seq"), lax.axis_index("vocab")
        self.s, self.v = s, v
        self.z, self.y = lax.div(s, NY), lax.rem(s, NY)
        self.x, self.c = lax.div(v, 2), lax.rem(v, 2)

    def yy(self, d):
        return lax.rem(self.y + d + NY, NY)

    def zz(self, d):
        return lax.rem(self.z + d + NZ, NZ)

    def xx(self, d):
        return lax.rem(self.x + d + NX, NX)

    def at_z(self, d):
        return (self.zz(d) * NY + self.y, self.v)

    def at_y(self, d):
        return (self.z * NY + self.yy(d), self.v)

    def at_x(self, d, core):
        return (self.s, self.xx(d) * 2 + core)

    def at_v(self, d):
        return (self.s, lax.rem(self.v + d, NV))


def rdma(src, dst, send, recv, dev):
    return pltpu.make_async_remote_copy(
        src_ref=src, dst_ref=dst, send_sem=send, recv_sem=recv, device_id=dev, device_id_type=MESH
    )


def greet(partners):
    bar = pltpu.get_barrier_semaphore()
    for dev in partners:
        pl.semaphore_signal(bar, inc=1, device_id=dev, device_id_type=MESH)


def gather_start(me, go, buf, zs, zr):
    own = buf.at[me.y, me.z]
    for d in (1, 7, 2, 6, 3, 5, 4):
        go(rdma(own, own, zs.at[d - 1], zr.at[me.z], me.at_z(d)))


def gather_pass(me, go, buf, src, own, zs, zr, ys, yr, order=(2, 1, 3)):
    blk = buf.at[me.y, src]
    if not own:
        rdma(blk, blk, zs.at[0], zr.at[src], me.at_z(1)).wait_recv()
    for e in order:
        go(rdma(blk, blk, ys.at[e - 1, src], yr.at[e - 1, src], me.at_y(e)))


def gather_wait(me, buf, e, src, ys, yr):
    blk = buf.at[me.yy(-e), src]
    rdma(blk, blk, ys.at[e - 1, src], yr.at[e - 1, src], me.at_y(e)).wait_recv()


PIECES = 4
TICKS = [(step, p) for step in range(NZ // 2 - 1) for p in range(PIECES)]
TICKS += [(NZ // 2 - 1, p) for p in range(PIECES // 2)]


def ring_piece(me, buf, k, way, step, p):
    rows = buf.shape[1] // PIECES
    p = p + k * (PIECES // 2) if step == NZ // 2 - 1 else p
    return buf.at[me.zz(-way * step), pl.ds(p * rows, rows)], p


def ring_tick(me, go, tick, buf, ss, rs):
    step, p0 = TICKS[tick]
    for k, way in ((0, 1), (1, -1)):
        blk, p = ring_piece(me, buf, k, way, step, p0)
        if step:
            rdma(blk, blk, ss.at[k, 0], rs.at[k, (step - 1) * PIECES + p], me.at_z(way)).wait_recv()
        go(rdma(blk, blk, ss.at[k, tick], rs.at[k, step * PIECES + p], me.at_z(way)))


def ring_wait(me, buf, ss, rs):
    last = NZ // 2 - 1
    rows = buf.shape[1] // PIECES
    for k, way in ((0, 1), (1, -1)):
        for p in range(PIECES):
            if p // (PIECES // 2) == k:
                blk = buf.at[me.zz(-way * (last + 1)), pl.ds(p * rows, rows)]
                rdma(blk, blk, ss.at[k, 0], rs.at[k, last * PIECES + p], me.at_z(way)).wait_recv()
            else:
                blk = buf.at[me.zz(-way * last), pl.ds(p * rows, rows)]
                rdma(blk, blk, ss.at[k, 0], rs.at[k, (last - 1) * PIECES + p], me.at_z(way)).wait_recv()


def lanes(shape):
    return lax.broadcasted_iota(jnp.int32, shape, len(shape) - 1)


def pack_lse(lse, low8):
    second = pltpu.roll(lse, 8, 1) if low8 else lse
    third = pltpu.roll(lse, 16, 1) if low8 else lse

    def split(a):
        hi = a.astype(BF).astype(F32)
        mid = (a - hi).astype(BF).astype(F32)
        return hi, mid, a - hi - mid

    lane = lanes(lse.shape)
    out = jnp.where(lane < 8, split(lse)[0], jnp.where(lane < 16, split(second)[1], split(third)[2]))
    return jnp.where(lane < 24, out, 0.0).astype(BF)


def unpack_lse(packed):
    a = packed.astype(F32)
    return a + (pltpu.roll(a, 120, 1) + pltpu.roll(a, 112, 1))


def join_partials(items, final=False):
    lses = [unpack_lse(it[:, GW:]) for it in items]
    peak = functools.reduce(jnp.maximum, lses)
    weights = [jnp.exp2(l - peak) for l in lses]
    total = functools.reduce(jnp.add, weights)
    weights = [w / total for w in weights]
    cols = []
    for h in range(HEADS):
        acc = None
        for w, it in zip(weights, items):
            term = w[:, h : h + 1] * it[:, h * HS : (h + 1) * HS].astype(F32)
            acc = term if acc is None else acc + term
        cols.append(acc.astype(BF))
    if not final:
        cols.append(pack_lse(peak + jnp.log2(total), True))
    return jnp.concatenate(cols, axis=1)


def kernel(
    q_ref, sk_ref, sv_ref, ck_ref, cv_ref, start_ref, w_ref, res_hbm, gain_hbm, hw_hbm, tgt_hbm,
    hid_ref, out_ref,
    qall, kbuf, vbuf, vext, bias, lse_buf, opart, ry, mg, rz, wall, hw_ref, res_ref, gain_ref, tgt_ref, tin, aall, ppart, rp, sq, nall, scy, scz, scale_of,
    osend, orecv, own, final, sx, x2, tgt_of, st_of, sty, stz,
    loc, kvs, kr, vr, gz, gzr, gy, gyr, ws, wr, rys, ryr, rzs, rzr, avs, avr, ps_, pr_, sqs, sqr, scs, scr, sczs, sczr,
    hz, hzr, hy, hyr, cs, cr, xs, xr, yss, yrs, zss, zrs,
):
    me = Place()
    sends = []

    def go(cp):
        cp.start()
        sends.append(cp)

    def cols(vv):
        return pl.ds(pl.multiple_of(vv * HS, HS), HS)

    def rows(vv):
        return pl.ds(pl.multiple_of(vv * CACHE, CACHE), CACHE)

    greet(
        [me.at_z(d) for d in range(1, NZ)]
        + [
            (me.z * NY + me.yy(dy), lax.rem(me.v + dv, NV))
            for dy in range(NY)
            for dv in range(NV)
            if dy or dv
        ]
    )

    def fetch(src, dst, sem):
        cp = pltpu.make_async_copy(src, dst, sem)
        cp.start()
        return cp

    head_cols = pl.ds(pl.multiple_of(me.v * GW, GW), GW)
    own_q = fetch(q_ref.at[:, head_cols], qall.at[me.y, me.z], loc.at[0])
    own_w = fetch(w_ref, wall.at[me.z], loc.at[1])
    own_k = fetch(ck_ref.at[:, cols(me.v)], kbuf.at[rows(me.v)], kr.at[me.v])
    own_v = fetch(cv_ref.at[:, cols(me.v)], vbuf.at[rows(me.v)], vr.at[me.v])
    span_k = fetch(sk_ref.at[:, cols(me.v)], kbuf.at[pl.ds(KEYS, ROWS)], loc.at[3])
    span_v = fetch(sv_ref.at[:, cols(me.v)], vbuf.at[pl.ds(KEYS, ROWS)], loc.at[4])
    later = [fetch(hw_hbm, hw_ref, loc.at[2]), fetch(res_hbm, res_ref, loc.at[5])]
    later += [fetch(gain_hbm, gain_ref, loc.at[6]), fetch(tgt_hbm, tgt_ref, loc.at[7])]
    kbuf[KEYS + ROWS :, :] = jnp.zeros((128 - ROWS, HS), BF)
    vbuf[KEYS + ROWS :, :] = jnp.zeros((128 - ROWS, HS), BF)
    flat = lanes((1, KEYS_PAD))
    bias[...] = jnp.where(flat < start_ref[0] - me.s * KEYS, 0.0, BIG_NEG)
    own_q.wait()
    own_w.wait()
    pl.semaphore_wait(pltpu.get_barrier_semaphore(), NZ - 1 + NY * NV - 1)

    gather_start(me, go, qall, gz, gzr)
    for i, d in enumerate((4, 3, 5, 2, 6, 1, 7)):
        vv = lax.rem(me.v + d, NV)
        go(rdma(ck_ref.at[:, cols(vv)], kbuf.at[rows(me.v)], kvs.at[0, i], kr.at[me.v], me.at_v(d)))
        go(rdma(cv_ref.at[:, cols(vv)], vbuf.at[rows(me.v)], kvs.at[1, i], vr.at[me.v], me.at_v(d)))
    ring_tick(me, go, 0, wall, ws, wr)
    ring_tick(me, go, 1, wall, ws, wr)
    for d in (0, 1, 7, 2, 6, 3, 5, 4):
        gather_pass(me, go, qall, me.zz(d), d == 0, gz, gzr, gy, gyr)
    ring_tick(me, go, 2, wall, ws, wr)
    ring_tick(me, go, 3, wall, ws, wr)
    span_k.wait()
    span_v.wait()
    own_k.wait()
    own_v.wait()
    for d in range(1, NV):
        src = lax.rem(me.v + d, NV)
        blk = kbuf.at[rows(src)]
        rdma(blk, blk, kvs.at[0, 0], kr.at[src], me.at_v(1)).wait_recv()
        blk = vbuf.at[rows(src)]
        rdma(blk, blk, kvs.at[1, 0], vr.at[src], me.at_v(1)).wait_recv()
    vext[:, :HS] = vbuf[...]
    vext[:, HS:] = jnp.ones((KEYS_PAD, HS), BF)
    ring_tick(me, go, 4, wall, ws, wr)

    scale = math.log2(math.e) / math.sqrt(HS)
    nrow = NZ * ROWS
    for turn, order in enumerate((2, 1, 3, 0)):
        yy = me.yy(order)
        if order:
            for d in (0, 1, 7, 2, 6, 3, 5, 4):
                gather_wait(me, qall, NY - order, me.zz(d), gy, gyr)

        def pair(hp):
            both = []
            for i in range(2):
                at = pl.ds((hp * 2 + i) * HS, HS)
                both.append(qall[yy, :, :, at].reshape(nrow, HS))
            q2 = jnp.concatenate(both, axis=0)
            sc = lax.dot_general(q2, kbuf[...], (((1,), (1,)), ((), ())), preferred_element_type=F32)
            main = sc[:, :KEYS] * scale + bias[:, :KEYS]
            row = lax.broadcasted_iota(jnp.int32, (2 * nrow, 128), 0)
            row = lax.rem(row, nrow)
            token = lax.div(row, ROWS) * (NY * ROWS) + yy * ROWS + lax.rem(row, ROWS)
            key = lanes((2 * nrow, 128))
            ok = (key < ROWS) & (key + me.s * ROWS <= token)
            span = jnp.where(ok, sc[:, KEYS:] * scale, BIG_NEG)
            peak = jnp.maximum(
                jnp.max(main, axis=1, keepdims=True), jnp.max(span, axis=1, keepdims=True)
            )
            pm = jnp.exp2(main - peak).astype(BF)
            ps = jnp.exp2(span - peak).astype(BF)
            ps = jnp.where(ok, ps, jnp.zeros_like(ps))
            o = jnp.dot(pm, vext[:KEYS, :], preferred_element_type=F32)
            o = o + jnp.dot(ps, vext[KEYS:, :], preferred_element_type=F32)
            total = o[:, HS:]
            total = jnp.where(total > 0.0, total, 1.0)
            on = (o[:, :HS] / total).astype(BF)
            lse = peak + jnp.log2(total)
            lane = lanes((nrow, 128))
            for i in range(2):
                h = hp * 2 + i
                at = pl.ds(h * HS, HS)
                opart[yy, :, :, at] = on[i * nrow : (i + 1) * nrow].reshape(NZ, ROWS, HS)
                mine = lse[i * nrow : (i + 1) * nrow]
                lse_buf[...] = jnp.where(lax.rem(lane, 8) == h, mine, lse_buf[...])

        def ship(part):
            at = pl.ds(0, GW // 2) if part == 0 else pl.ds(GW // 2, PW - GW // 2)
            src, dst = opart.at[yy, :, :, at], ry.at[order - 1, :, :, at]
            go(rdma(src, dst, rys.at[part, order - 1], ryr.at[part, order - 1], me.at_y(order)))

        pair(0)
        pair(1)
        if order:
            ship(0)
        ring_tick(me, go, 5 + turn, wall, ws, wr)
        pair(2)
        pair(3)
        opart[yy, :, :, GW:] = pack_lse(lse_buf[...], False).reshape(NZ, ROWS, 128)
        if order:
            ship(1)

    ring_tick(me, go, 9, wall, ws, wr)
    ring_tick(me, go, 10, wall, ws, wr)
    items = [opart[me.y].reshape(nrow, PW)]
    for d in (2, 1, 3):
        for part, at in ((0, pl.ds(0, GW // 2)), (1, pl.ds(GW // 2, PW - GW // 2))):
            blk = ry.at[d - 1, :, :, at]
            rdma(blk, blk, rys.at[part, d - 1], ryr.at[part, d - 1], me.at_y(d)).wait_recv()
        items.append(ry[d - 1].reshape(nrow, PW))
    mg[...] = join_partials(items).reshape(NZ, ROWS, PW)
    for d in (4, 3, 5, 2, 6, 1, 7):
        go(rdma(mg.at[me.zz(d)], rz.at[d - 1], rzs.at[d - 1], rzr.at[d - 1], me.at_z(d)))
    ring_tick(me, go, 11, wall, ws, wr)
    items = [mg[me.z]]
    for d in range(1, NZ):
        blk = rz.at[d - 1]
        rdma(blk, blk, rzs.at[d - 1], rzr.at[d - 1], me.at_z(d)).wait_recv()
        items.append(rz[d - 1])
    att = join_partials(items, final=True)
    ring_tick(me, go, 12, wall, ws, wr)
    ring_tick(me, go, 13, wall, ws, wr)

    plane = [(dy, dv) for dv in (4, 3, 5, 2, 6, 1, 7, 0) for dy in (2, 1, 3, 0)][:-1]
    for j in range(NY):
        tin[0, j] = att[:, j * FEAT : (j + 1) * FEAT]
    aall[me.v, me.y] = tin[0, me.y]
    for dy, dv in plane:
        dev = (me.z * NY + me.yy(dy), lax.rem(me.v + dv, NV))
        go(rdma(tin.at[0, me.yy(dy)], aall.at[me.v, me.y], avs.at[dv, dy], avr.at[dv, dy], dev))
    tok = NY * ROWS
    for dy, dv in reversed(plane):
        blk = aall.at[lax.rem(me.v - dv + NV, NV), me.yy(-dy)]
        rdma(blk, blk, avs.at[dv, dy], avr.at[dv, dy], me.at_y(1)).wait_recv()
    ring_wait(me, wall, ws, wr)
    lhs = jnp.concatenate([aall[g].reshape(tok, FEAT) for g in range(NV)], axis=1)
    proj = jnp.dot(lhs, wall[...].reshape(NV * FEAT, GW), preferred_element_type=F32)
    ppart[...] = proj.astype(BF).reshape(NY, ROWS, GW)
    for d in (2, 1, 3):
        go(rdma(ppart.at[me.yy(d)], rp.at[d - 1], ps_.at[d - 1], pr_.at[d - 1], me.at_y(d)))
    for cp in later[1:3]:
        cp.wait()
    total = res_ref[...].astype(F32) + ppart[me.y].astype(F32)
    for d in (1, 3, 2):
        blk = rp.at[d - 1]
        rdma(blk, blk, ps_.at[d - 1], pr_.at[d - 1], me.at_y(d)).wait_recv()
        total = total + rp[d - 1].astype(F32)
    hidden = total.astype(BF)
    hid_ref[...] = hidden

    nall[me.y, me.z] = hidden
    gather_start(me, go, nall, hz, hzr)
    wide = hidden.astype(F32)
    sq[me.v] = jnp.broadcast_to(jnp.sum(wide * wide, axis=1, keepdims=True), (ROWS, 128))
    for d in (4, 3, 5, 2, 6, 1, 7):
        go(rdma(sq.at[me.v], sq.at[me.v], sqs.at[d - 1], sqr.at[d - 1], me.at_v(d)))
    gather_pass(me, go, nall, me.z, True, hz, hzr, hy, hyr, (1, 3, 2))
    for d in range(1, NV):
        blk = sq.at[lax.rem(me.v - d + NV, NV)]
        rdma(blk, blk, sqs.at[d - 1], sqr.at[d - 1], me.at_v(1)).wait_recv()
    mean = jnp.sum(sq[...], axis=0) * (1.0 / D)
    spread = jnp.transpose(jnp.concatenate([lax.rsqrt(mean + EPSILON)] * (128 // ROWS), axis=0))[:8]
    scy[0] = jnp.where(lax.div(lanes((8, 128)), ROWS) == me.y, spread, 0.0)
    for d in (2, 1, 3):
        go(rdma(scy.at[0], scy.at[d], scs.at[d - 1], scr.at[d - 1], me.at_y(d)))
    for d in (1, 7):
        gather_pass(me, go, nall, me.zz(d), False, hz, hzr, hy, hyr, (1, 3, 2))
    for d in (2, 1, 3):
        rdma(scy.at[d], scy.at[d], scs.at[d - 1], scr.at[d - 1], me.at_y(d)).wait_recv()
    scz[me.z] = scy[0] + scy[1] + scy[2] + scy[3]
    for d in (4, 3, 5, 2, 6, 1, 7):
        go(rdma(scz.at[me.z], scz.at[me.z], sczs.at[d - 1], sczr.at[me.z], me.at_z(d)))
    for d in (2, 6, 3, 5, 4):
        gather_pass(me, go, nall, me.zz(d), False, hz, hzr, hy, hyr, (1, 3, 2))
    for d in range(1, NZ):
        blk = scz.at[me.zz(d)]
        rdma(blk, blk, sczs.at[0], sczr.at[me.zz(d)], me.at_z(1)).wait_recv()
    turned = [scz[i, 0:1] for i in range(NZ)] + [jnp.zeros((128 - NZ, 128), F32)]
    scale_of[...] = jnp.transpose(jnp.concatenate(turned, axis=0))
    for cp in later[:1] + later[3:]:
        cp.wait()

    shift = (2, 1, 3, 0)

    def multiply(o):
        yy = me.yy(-o)
        if o:
            for d in (0, 1, 7, 2, 6, 3, 5, 4):
                gather_wait(me, nall, o, me.zz(d), hy, hyr)
        scales = scale_of[pl.ds(pl.multiple_of(yy * ROWS, ROWS), ROWS)]
        blocks = []
        for core in (1 - me.c, me.c):
            for d in shift:
                zz = me.xx(d) * 2 + core
                rs = jnp.where(lanes((ROWS, 128)) == zz, scales, 0.0)
                rs = jnp.sum(rs, axis=1, keepdims=True)
                blocks.append((nall[yy, zz].astype(F32) * rs * gain_ref[...]).astype(BF))
        lhs = jnp.concatenate(blocks, axis=0)
        for n in range(NT):
            at = pl.ds(n * TILE, TILE)
            both = jnp.dot(lhs, hw_ref[:, at], preferred_element_type=F32)
            osend[o, :, :, at] = both[:tok].astype(BF).reshape(NX, ROWS, TILE)
            own[o, :, :, at] = both[tok:].reshape(NX, ROWS, TILE)
        go(rdma(osend.at[o], orecv.at[o], cs.at[o], cr.at[o], me.at_x(0, 1 - me.c)))

    def pass_on(o):
        rdma(orecv.at[o], orecv.at[o], cs.at[o], cr.at[o], me.at_x(0, 1 - me.c)).wait_recv()
        for i, d in enumerate(shift[:3]):
            sx[o, i] = (own[o, i] + orecv[o, i].astype(F32)).astype(BF)
            go(rdma(sx.at[o, i], x2.at[o, i], xs.at[o, i], xr.at[o, i], me.at_x(d, me.c)))
        at = pl.ds(pl.multiple_of(me.yy(-o) * ROWS, ROWS), ROWS)
        final[at] = own[o, 3] + orecv[o, 3].astype(F32)

    tgt = jnp.concatenate([tgt_ref[...], jnp.zeros((1, 128 - tok), jnp.int32)], axis=1)
    tgt = jnp.transpose(jnp.broadcast_to(tgt.astype(F32), (128, 128)))
    tgt_of[...] = tgt[:tok].astype(jnp.int32) - me.s * VOC

    turns = (0, 1, 3, 2)
    multiply(turns[0])
    for before, o in zip(turns, turns[1:]):
        pass_on(before)
        multiply(o)
    pass_on(turns[3])

    lane = lanes((ROWS, 128))
    for o in turns:
        at = pl.ds(pl.multiple_of(me.yy(-o) * ROWS, ROWS), ROWS)
        lg = final[at]
        for i in range(3):
            rdma(x2.at[o, i], x2.at[o, i], xs.at[o, i], xr.at[o, i], me.at_x(1, me.c)).wait_recv()
            lg = lg + x2[o, i].astype(F32)
        peak = jnp.max(lg, axis=1, keepdims=True)
        total = jnp.sum(jnp.exp(lg - peak), axis=1, keepdims=True)
        hit = lanes((ROWS, VOC)) == tgt_of[at][:, :1]
        picked = jnp.sum(jnp.where(hit, lg, 0.0), axis=1, keepdims=True)
        st_of[at] = jnp.where(lane == 0, peak, jnp.where(lane == 1, total, picked))
    st = jnp.concatenate([st_of[...], jnp.zeros((128 - tok, 128), F32)], axis=0)
    sty[0] = jnp.transpose(st)[:8]

    def joined(buf, count):
        top = functools.reduce(jnp.maximum, [buf[i, 0:1] for i in range(count)])
        tot = functools.reduce(jnp.add, [buf[i, 1:2] * jnp.exp(buf[i, 0:1] - top) for i in range(count)])
        pick = functools.reduce(jnp.add, [buf[i, 2:3] for i in range(count)])
        return top, tot, pick

    for d in (2, 1, 3):
        go(rdma(sty.at[0], sty.at[d], yss.at[d - 1], yrs.at[d - 1], me.at_y(d)))
    for d in range(1, NY):
        rdma(sty.at[d], sty.at[d], yss.at[d - 1], yrs.at[d - 1], me.at_y(d)).wait_recv()
    top, tot, pick = joined(sty, NY)
    stz[0] = jnp.concatenate([top, tot, pick, jnp.zeros((5, 128), F32)], axis=0)
    for d in (4, 3, 5, 2, 6, 1, 7):
        go(rdma(stz.at[0], stz.at[d], zss.at[d - 1], zrs.at[d - 1], me.at_z(d)))
    for d in range(1, NZ):
        rdma(stz.at[d], stz.at[d], zss.at[d - 1], zrs.at[d - 1], me.at_z(d)).wait_recv()
    top, tot, pick = joined(stz, NZ)
    out_ref[...] = (pick - (top + jnp.log(tot)))[:, :tok]
    for cp in sends:
        cp.wait_send()


def hand_over(hid_ref, logprob_ref, hid_out, logprob_out):
    hid_out[...] = hid_ref[...]
    logprob_out[...] = logprob_ref[0, :]


def vm():
    return pl.BlockSpec(memory_space=pltpu.VMEM)


def params(cid):
    return pltpu.CompilerParams(
        collective_id=cid, has_side_effects=True, vmem_limit_bytes=56 * 1024 * 1024
    )


def dma(*shape):
    return pltpu.SemaphoreType.DMA(shape)


def shards(q, sk, sv, ck, cv, start, w, res, gain, hw, tgt):
    any_ = pl.BlockSpec(memory_space=pl.ANY)
    tok = NY * ROWS
    hidden, logprobs = pl.pallas_call(
        kernel,
        out_shape=(
            jax.ShapeDtypeStruct((ROWS, GW), BF),
            jax.ShapeDtypeStruct((1, tok), F32),
        ),
        in_specs=[any_] * 5 + [pl.BlockSpec(memory_space=pltpu.SMEM)] + [any_] * 5,
        out_specs=(vm(), vm()),
        scratch_shapes=[
            pltpu.VMEM((NY, NZ, ROWS, GW), BF),
            pltpu.VMEM((KEYS_PAD, HS), BF),
            pltpu.VMEM((KEYS_PAD, HS), BF),
            pltpu.VMEM((KEYS_PAD, 2 * HS), BF),
            pltpu.VMEM((1, KEYS_PAD), F32),
            pltpu.VMEM((NZ * ROWS, 128), F32),
            pltpu.VMEM((NY, NZ, ROWS, PW), BF),
            pltpu.VMEM((NY - 1, NZ, ROWS, PW), BF),
            pltpu.VMEM((NZ, ROWS, PW), BF),
            pltpu.VMEM((NZ - 1, ROWS, PW), BF),
            pltpu.VMEM((NZ, FEAT, GW), BF),
            pltpu.VMEM((GW, VOC), BF),
            pltpu.VMEM((ROWS, GW), BF),
            pltpu.VMEM((1, GW), F32),
            pltpu.VMEM((1, tok), jnp.int32),
            pltpu.VMEM((1, NY, ROWS, FEAT), BF),
            pltpu.VMEM((NV, NY, ROWS, FEAT), BF),
            pltpu.VMEM((NY, ROWS, GW), BF),
            pltpu.VMEM((NY - 1, ROWS, GW), BF),
            pltpu.VMEM((NV, ROWS, 128), F32),
            pltpu.VMEM((NY, NZ, ROWS, GW), BF),
            pltpu.VMEM((NY, 8, 128), F32),
            pltpu.VMEM((NZ, 8, 128), F32),
            pltpu.VMEM((128, 128), F32),
            pltpu.VMEM((NY, NX, ROWS, VOC), BF),
            pltpu.VMEM((NY, NX, ROWS, VOC), BF),
            pltpu.VMEM((NY, NX, ROWS, VOC), F32),
            pltpu.VMEM((tok, VOC), F32),
            pltpu.VMEM((NY, NX - 1, ROWS, VOC), BF),
            pltpu.VMEM((NY, NX - 1, ROWS, VOC), BF),
            pltpu.VMEM((tok, 128), jnp.int32),
            pltpu.VMEM((tok, 128), F32),
            pltpu.VMEM((NY, 8, 128), F32),
            pltpu.VMEM((NZ, 8, 128), F32),
            dma(8), dma(2, NV - 1), dma(NV), dma(NV),
            dma(NZ - 1), dma(NZ), dma(NY - 1, NZ), dma(NY - 1, NZ),
            dma(2, len(TICKS)), dma(2, NZ // 2 * PIECES),
            dma(2, NY - 1), dma(2, NY - 1), dma(NZ - 1), dma(NZ - 1),
            dma(NV, NY), dma(NV, NY),
            dma(NY - 1), dma(NY - 1), dma(NV - 1), dma(NV - 1),
            dma(NY - 1), dma(NY - 1), dma(NZ - 1), dma(NZ),
            dma(NZ - 1), dma(NZ), dma(NY - 1, NZ), dma(NY - 1, NZ),
            dma(NY), dma(NY), dma(NY, NX - 1), dma(NY, NX - 1),
            dma(NY - 1), dma(NY - 1), dma(NZ - 1), dma(NZ - 1),
        ],
        compiler_params=params(0),
        name="layer",
    )(q, sk, sv, ck, cv, start, w, res, gain.reshape(1, GW), hw, tgt.reshape(1, tok))
    return pl.pallas_call(
        hand_over,
        out_shape=(jax.ShapeDtypeStruct((ROWS, GW), BF), jax.ShapeDtypeStruct((tok,), F32)),
        in_specs=[vm(), vm()],
        out_specs=(vm(), vm()),
        name="results",
    )(hidden, logprobs)


def solution(mesh):
    placed = (
        P("seq", None),
        P("seq", None),
        P("seq", None),
        P(("seq", "vocab"), None),
        P(("seq", "vocab"), None),
        P(),
        P("seq", "vocab"),
        P("seq", "vocab"),
        P("vocab"),
        P("vocab", "seq"),
        P("vocab"),
    )
    return jax.shard_map(
        shards,
        mesh=mesh,
        in_specs=placed,
        out_specs=(P("seq", "vocab"), P("vocab")),
        check_vma=False,
    )
```
